32 devices in a mesh: section: 2 (over core), row: 4 (over z), col: 4 (over y, x).
Axes of the slice: x: 2, y: 2, z: 4, core: 2. Of those that a mesh axis runs over, the one named last changes fastest.
Arguments:
- block_input: bfloat16 [4, 1600, 2048], P(None, 'col', 'row'), may hold values from -6 to 6
- out_cotangent: bfloat16 [4, 1600, 2048], P(None, 'col', 'row'), may hold values from -6 to 6
- group_order: int32 [8], replicated, may hold values from 0 to 7, each once
- first_gain: float32 [2, 1600], P('section', 'col'), may hold values from 0.1 to 1.9
- first_bias: float32 [2, 1600], P('section', 'col'), may hold values from -4 to 4
- query_weight: bfloat16 [2, 1600, 1600], P('section', 'row', 'col'), may hold values from -0.15625 to 0.15625
- key_weight: bfloat16 [2, 1600, 1600], P('section', 'row', 'col'), may hold values from -0.15625 to 0.15625
- value_weight: bfloat16 [2, 1600, 1600], P('section', 'row', 'col'), may hold values from -0.15625 to 0.15625
- query_bias: float32 [2, 1600], P('section', 'col'), may hold values from -4 to 4
- value_bias: float32 [2, 1600], P('section', 'col'), may hold values from -4 to 4
- out_weight: bfloat16 [2, 1600, 1600], P('section', 'col', 'row'), may hold values from -1.25 to 1.25
- out_bias: float32 [2, 1600], P('section', 'col'), may hold values from -4 to 4
- second_gain: float32 [2, 1600], P('section', 'col'), may hold values from 0.1 to 1.9
- second_bias: float32 [2, 1600], P('section', 'col'), may hold values from -4 to 4
- up_weight: bfloat16 [2, 1600, 6400], P('section', 'row', 'col'), may hold values from -0.15625 to 0.15625
- up_bias: float32 [2, 6400], P('section', 'col'), may hold values from -4 to 4
- down_weight: bfloat16 [2, 1600, 6400], P('section', 'row', 'col'), may hold values from -0.078125 to 0.078125
- down_bias: float32 [2, 1600], P('section', 'col'), may hold values from -4 to 4
Outputs:
- boundary: float32 [2, 4, 1600, 2048], P('section', None, 'col', 'row')
- first_gain_gradient: float32 [2, 1600], P('section', 'col')
- first_bias_gradient: float32 [2, 1600], P('section', 'col')
- query_weight_gradient: float32 [2, 1600, 1600], P('section', 'row', 'col')
- key_weight_gradient: float32 [2, 1600, 1600], P('section', 'row', 'col')
- value_weight_gradient: float32 [2, 1600, 1600], P('section', 'row', 'col')
- query_bias_gradient: float32 [2, 1600], P('section', 'col')
- value_bias_gradient: float32 [2, 1600], P('section', 'col')
- out_weight_gradient: float32 [2, 1600, 1600], P('section', 'col', 'row')
- out_bias_gradient: float32 [2, 1600], P('section', 'col')
- second_gain_gradient: float32 [2, 1600], P('section', 'col')
- second_bias_gradient: float32 [2, 1600], P('section', 'col')
- up_weight_gradient: float32 [2, 1600, 6400], P('section', 'row', 'col')
- up_bias_gradient: float32 [2, 6400], P('section', 'col')
- down_weight_gradient: float32 [2, 1600, 6400], P('section', 'row', 'col')
- down_bias_gradient: float32 [2, 1600], P('section', 'col')
The draws below stay inside these ranges and needn't reach their ends.
Inputs may be any that keep to these rules, and one draw needn't show every extreme that they name: `group_order`: a permutation of 0 to 7, the same for every sequence.
All inputs are finite; a program needn't handle non-finite values.
Results may differ from the reference program's by a relative error of at most 0.015.
Values may be sent and summed in bfloat16 or wider, within the bound.
No kernel may reach another device: no remote copies, remote signals or barrier semaphores. Data moves between devices by JAX's collectives and lax.ppermute only.
A program may use at most 448 MiB of HBM per device.

```python
import math
import jax
import jax.numpy as jnp
from jax import lax

D = 1600
H = 25
HD = 64
FF = 6400
L = 512
M = 4
SEQ = 4
NCHUNK = 8


def block_scale(own_key, dims, cuts, least, largest):
    level, own = 1.0, jax.random.fold_in(own_key, 6)
    for axis_at, blocks in cuts:
        steps = jnp.exp(jax.random.uniform(jax.random.fold_in(own, axis_at), (blocks,), jnp.float32, least / len(cuts), largest / len(cuts)))
        level = level * jnp.repeat(steps, dims[axis_at] // blocks).reshape([-1 if axis == axis_at else 1 for axis in range(len(dims))])
    return level


def noise(rng, dims, width, limit, split=(), kind=jnp.bfloat16):
    drawn = width * jax.random.normal(rng, dims, jnp.float32)
    if split:
        drawn = drawn * block_scale(rng, dims, split, -0.22, 0.18)
    return jnp.clip(drawn, -limit, limit).astype(kind)


def setup_inputs(seed: int = 0) -> dict:
    key_list = jax.random.split(jax.random.key(seed), 19)
    return {
        "block_input": noise(key_list[0], (M, D, SEQ * L), 1.0, 6.0, ((1, 4), (2, 4))),
        "out_cotangent": noise(key_list[1], (M, D, SEQ * L), 1.0, 6.0, ((1, 4), (2, 4))),
        "group_order": jax.random.permutation(key_list[2], NCHUNK).astype(jnp.int32),
        "first_gain": jnp.clip(1.0 + 0.18 * jax.random.normal(key_list[3], (2, D), jnp.float32), 0.1, 1.9),
        "first_bias": noise(key_list[4], (2, D), 1.0, 4.0, ((0, 2), (1, 4)), jnp.float32),
        "query_weight": noise(key_list[5], (2, D, D), D ** -0.5, 0.15625, ((0, 2), (1, 4), (2, 4))),
        "key_weight": noise(key_list[6], (2, D, D), D ** -0.5, 0.15625, ((0, 2), (1, 4), (2, 4))),
        "value_weight": noise(key_list[7], (2, D, D), D ** -0.5, 0.15625, ((0, 2), (1, 4), (2, 4))),
        "query_bias": noise(key_list[8], (2, D), 1.0, 4.0, ((0, 2), (1, 4)), jnp.float32),
        "value_bias": noise(key_list[9], (2, D), 1.0, 4.0, ((0, 2), (1, 4)), jnp.float32),
        "out_weight": noise(key_list[10], (2, D, D), (max(D // 64, 1)) ** -0.5, 1.25, ((0, 2), (1, 4), (2, 4))),
        "out_bias": noise(key_list[11], (2, D), 1.0, 4.0, ((0, 2), (1, 4)), jnp.float32),
        "second_gain": jnp.clip(1.0 + 0.18 * jax.random.normal(key_list[12], (2, D), jnp.float32), 0.1, 1.9),
        "second_bias": noise(key_list[13], (2, D), 1.0, 4.0, ((0, 2), (1, 4)), jnp.float32),
        "up_weight": noise(key_list[14], (2, D, FF), D ** -0.5, 0.15625, ((0, 2), (1, 4), (2, 4))),
        "up_bias": noise(key_list[15], (2, FF), 1.0, 4.0, ((0, 2), (1, 4)), jnp.float32),
        "down_weight": noise(key_list[16], (2, D, FF), FF ** -0.5, 0.078125, ((0, 2), (1, 4), (2, 4))),
        "down_bias": noise(key_list[17], (2, D), 1.0, 4.0, ((0, 2), (1, 4)), jnp.float32),
    }


epsilon = 1e-05
tanh_scale = math.sqrt(2.0 / math.pi)
cubic_weight = 0.044715

def gelu_value(inputs):
    inner = tanh_scale * (inputs + cubic_weight * inputs * inputs * inputs)
    return 0.5 * inputs * (1.0 + jnp.tanh(inner))

def gelu_slope(inputs):
    inner = tanh_scale * (inputs + cubic_weight * inputs * inputs * inputs)
    tangent = jnp.tanh(inner)
    return 0.5 * (1.0 + tangent) + 0.5 * inputs * (1.0 - tangent * tangent) * tanh_scale * (1.0 + 3.0 * cubic_weight * inputs * inputs)

def matmul(left, right):
    return jnp.dot(left, right, preferred_element_type=jnp.float32)

def norm_forward(stream, gain, offset):
    row_mean = lax.optimization_barrier(jnp.mean(stream, axis=1, keepdims=True))
    row_scale = lax.rsqrt(lax.optimization_barrier(jnp.mean(stream * stream, axis=1, keepdims=True)) - row_mean * row_mean + epsilon)
    normed = (stream - row_mean) * row_scale
    return ((normed * gain + offset).astype(jnp.bfloat16), normed, row_scale)

def norm_backward(incoming, normed, row_scale, gain):
    scaled = incoming * gain
    outgoing = row_scale * (scaled - lax.optimization_barrier(jnp.mean(scaled, axis=1, keepdims=True)) - normed * lax.optimization_barrier(jnp.mean(scaled * normed, axis=1, keepdims=True)))
    return (outgoing, lax.optimization_barrier(jnp.sum(incoming * normed, axis=0)), lax.optimization_barrier(jnp.sum(incoming, axis=0)))

def split_heads(values):
    return values.astype(jnp.float32).reshape(values.shape[0], H, HD)

def attention_scores(queries, key_rows, allowed):
    logits = jnp.einsum('qhd,khd->hqk', split_heads(queries), split_heads(key_rows)) * HD ** (-0.5)
    return jnp.where(allowed[None], logits, -jnp.inf)

def layer_forward(stream, params, allowed):
    gain_one, bias_one, query_full, key_full, value_full, query_shift, value_shift, out_full, out_shift, gain_two, bias_two, up_full, up_shift, down_full, down_shift = params
    inputs_one, normed_one, scale_one = norm_forward(stream, gain_one, bias_one)
    queries = (matmul(inputs_one, query_full) + query_shift).astype(jnp.bfloat16)
    key_rows = matmul(inputs_one, key_full).astype(jnp.bfloat16)
    value_rows = (matmul(inputs_one, value_full) + value_shift).astype(jnp.bfloat16)
    scores = attention_scores(queries, key_rows, allowed)
    row_peak = lax.optimization_barrier(jnp.max(scores, axis=2, keepdims=True))
    log_total = row_peak + jnp.log(lax.optimization_barrier(jnp.sum(jnp.exp(scores - row_peak), axis=2, keepdims=True)))
    softmax_half = jnp.exp(scores - log_total).astype(jnp.bfloat16)
    attended = jnp.einsum('hqk,khd->qhd', softmax_half.astype(jnp.float32), split_heads(value_rows))
    attended = attended.astype(jnp.bfloat16).reshape(queries.shape)
    middle = stream + matmul(attended, out_full) + out_shift
    inputs_two, normed_two, scale_two = norm_forward(middle, gain_two, bias_two)
    hidden_pre = matmul(inputs_two, up_full) + up_shift
    hidden = gelu_value(hidden_pre).astype(jnp.bfloat16)
    result = middle + matmul(hidden, down_full.T) + down_shift
    saved = (normed_one, scale_one, inputs_one, queries, key_rows, value_rows, log_total, attended, normed_two, scale_two, inputs_two, hidden_pre, hidden)
    return (result, saved)

def layer_backward(upstream, saved, params, allowed):
    gain_one, bias_one, query_full, key_full, value_full, query_shift, value_shift, out_full, out_shift, gain_two, bias_two, up_full, up_shift, down_full, down_shift = params
    normed_one, scale_one, inputs_one, queries, key_rows, value_rows, log_total, attended, normed_two, scale_two, inputs_two, hidden_pre, hidden = saved
    upstream_half = upstream.astype(jnp.bfloat16)
    down_grad = matmul(upstream_half.T, hidden)
    down_shift_grad = lax.optimization_barrier(jnp.sum(upstream, axis=0))
    hidden_grad = matmul(upstream_half, down_full) * gelu_slope(hidden_pre)
    hidden_half = hidden_grad.astype(jnp.bfloat16)
    up_shift_grad = lax.optimization_barrier(jnp.sum(hidden_grad, axis=0))
    up_grad = matmul(inputs_two.T, hidden_half)
    middle_part, gain_two_grad, bias_two_grad = norm_backward(matmul(hidden_half, up_full.T), normed_two, scale_two, gain_two)
    middle_grad = upstream + middle_part
    middle_half = middle_grad.astype(jnp.bfloat16)
    out_shift_grad = lax.optimization_barrier(jnp.sum(middle_grad, axis=0))
    out_grad = matmul(attended.T, middle_half)
    attended_grad = matmul(middle_half, out_full.T).astype(jnp.bfloat16)
    scores = attention_scores(queries, key_rows, allowed)
    softmax_weights = jnp.exp(scores - log_total)
    softmax_half = softmax_weights.astype(jnp.bfloat16)
    grad_heads = split_heads(attended_grad)
    value_grad_rows = jnp.einsum('hqk,qhd->khd', softmax_half.astype(jnp.float32), grad_heads).reshape(value_rows.shape)
    probs_grad = jnp.einsum('qhd,khd->hqk', grad_heads, split_heads(value_rows))
    row_dot = lax.optimization_barrier(jnp.sum(softmax_weights * probs_grad, axis=2, keepdims=True))
    scores_grad = (softmax_weights * (probs_grad - row_dot) * HD ** (-0.5)).astype(jnp.bfloat16)
    query_half = jnp.einsum('hqk,khd->qhd', scores_grad.astype(jnp.float32), split_heads(key_rows))
    query_half = query_half.astype(jnp.bfloat16).reshape(queries.shape)
    key_grad_rows = jnp.einsum('hqk,qhd->khd', scores_grad.astype(jnp.float32), split_heads(queries)).reshape(key_rows.shape)
    key_half = key_grad_rows.astype(jnp.bfloat16)
    value_half = value_grad_rows.astype(jnp.bfloat16)
    query_shift_grad = lax.optimization_barrier(jnp.sum(query_half.astype(jnp.float32), axis=0))
    value_shift_grad = lax.optimization_barrier(jnp.sum(value_grad_rows, axis=0))
    query_grad = matmul(inputs_one.T, query_half)
    key_grad = matmul(inputs_one.T, key_half)
    value_grad = matmul(inputs_one.T, value_half)
    back_one = matmul(query_half, query_full.T) + matmul(key_half, key_full.T) + matmul(value_half, value_full.T)
    stream_part, gain_one_grad, bias_one_grad = norm_backward(back_one, normed_one, scale_one, gain_one)
    stream_grad = middle_grad + stream_part
    grads = (gain_one_grad, bias_one_grad, query_grad, key_grad, value_grad, query_shift_grad, value_shift_grad, out_grad, out_shift_grad, gain_two_grad, bias_two_grad, up_grad, up_shift_grad, down_grad, down_shift_grad)
    return (stream_grad, grads)

def reference(block_input, out_cotangent, group_order, first_gain, first_bias, query_weight, key_weight, value_weight, query_bias, value_bias, out_weight, out_bias, second_gain, second_bias, up_weight, up_bias, down_weight, down_bias):
    group_rows = L // NCHUNK
    row_ids = jnp.arange(L, dtype=jnp.int32)
    position = group_order[row_ids // group_rows] * group_rows + row_ids % group_rows
    allowed = position[None, :] <= position[:, None]
    params = (first_gain, first_bias, query_weight, key_weight, value_weight, query_bias, value_bias, out_weight, out_bias, second_gain, second_bias, up_weight, up_bias, down_weight, down_bias)
    layer_zero = tuple((piece[0] for piece in params))
    layer_one = tuple((piece[1] for piece in params))
    sequences = jnp.transpose(block_input, (0, 2, 1)).reshape(M * SEQ, L, D)
    cotangents = jnp.transpose(out_cotangent, (0, 2, 1)).reshape(M * SEQ, L, D)
    totals = tuple((jnp.zeros(piece.shape, jnp.float32) for piece in params))

    def visit(carry, pieces):
        seq_input, seq_cotangent = pieces
        middle_out, saved_zero = layer_forward(seq_input.astype(jnp.float32), layer_zero, allowed)
        final_out, saved_one = layer_forward(middle_out, layer_one, allowed)
        middle_grad, grads_one = layer_backward(seq_cotangent.astype(jnp.float32), saved_one, layer_one, allowed)
        input_grad, grads_zero = layer_backward(middle_grad, saved_zero, layer_zero, allowed)
        carry = tuple((total + jnp.stack([first_part, second_part]) for total, first_part, second_part in zip(carry, grads_zero, grads_one)))
        return (carry, (input_grad, final_out))
    totals, (input_grads, final_outs) = lax.scan(visit, totals, (sequences, cotangents))
    input_cols = jnp.transpose(input_grads.reshape(M, SEQ * L, D), (0, 2, 1))
    final_cols = jnp.transpose(final_outs.reshape(M, SEQ * L, D), (0, 2, 1))
    boundary = jnp.stack([input_cols, final_cols])
    return (boundary, totals[0], totals[1], totals[2], totals[3], totals[4], totals[5], totals[6], totals[7], totals[8], totals[9], totals[10], totals[11], totals[12], totals[13], totals[14])
```

```python
import functools
import math

import jax
import jax.numpy as jnp
from jax import lax
from jax.experimental import pallas as pl
from jax.experimental.pallas import tpu as pltpu
from jax.sharding import PartitionSpec as P

H = 25
HD = 64
L = 512
BF = jnp.bfloat16
F32 = jnp.float32

epsilon = 1e-05
tanh_scale = math.sqrt(2.0 / math.pi)
cubic_weight = 0.044715
score_scale = HD ** (-0.5)


def xor_step(value, axis, step):
    count = lax.axis_size(axis)
    return lax.ppermute(value, axis, [(i, i ^ step) for i in range(count)])


def gather_tokens(rows):
    count = lax.axis_size("col")
    return jnp.concatenate([rows] + [xor_step(rows, "col", j) for j in range(1, count)])


def scatter_terms(partial_rows):
    count = lax.axis_size("col")
    here = partial_rows.shape[0] // count
    terms = [partial_rows[:here]]
    for j in range(1, count):
        terms.append(xor_step(partial_rows[j * here : (j + 1) * here], "col", j))
    return terms


def total(terms):
    result = terms[0].astype(F32)
    for term in terms[1:]:
        result = result + term.astype(F32)
    return result


def swap_section(value):
    return xor_step(value, "section", 1)


def xor_order(stack, index):
    count = stack.shape[0]
    return jnp.stack(
        [lax.dynamic_index_in_dim(stack, index ^ t, 0, keepdims=False) for t in range(count)]
    )


def head_share():
    count = lax.axis_size("col")
    return H // count, (H // count + 1) * HD


def head_shift(col_index):
    count = lax.axis_size("col")
    return jnp.where(col_index == 0, 0, HD - (HD // count) * col_index)


def align_heads(columns, col_index):
    count = lax.axis_size("col")
    per, wide = head_share()
    lead = columns.shape[:-1]
    after = lax.ppermute(columns[..., :HD], "col", [(i + 1, i) for i in range(count - 1)])
    own = columns.shape[-1]
    pad = max(0, wide + HD - own - HD)
    extended = jnp.concatenate([columns, after, jnp.zeros(lead + (pad,), columns.dtype)], axis=-1)
    moved = lax.dynamic_slice_in_dim(
        extended, head_shift(col_index), wide, axis=extended.ndim - 1
    )
    limit = jnp.where(col_index == 0, wide, per * HD)
    return jnp.where(jnp.arange(wide) < limit, moved, jnp.zeros((), moved.dtype))


def unalign_heads(columns, width, col_index):
    count = lax.axis_size("col")
    per, wide = head_share()
    shift = head_shift(col_index)
    after_shift = HD - (HD // count) * (col_index + 1)
    begin = width - shift
    padded = jnp.concatenate(
        [columns, jnp.zeros(columns.shape[:-1] + (HD,), columns.dtype)], axis=-1
    )
    tail = lax.dynamic_slice_in_dim(padded, begin, HD, axis=columns.ndim - 1)
    before = lax.ppermute(tail, "col", [(i, i + 1) for i in range(count - 1)])
    joined = jnp.concatenate([before, columns], axis=-1)
    rest = lax.dynamic_slice_in_dim(
        jnp.concatenate(
            [joined, jnp.zeros(columns.shape[:-1] + (HD,), columns.dtype)], axis=-1
        ),
        HD - shift,
        width,
        axis=columns.ndim - 1,
    )
    front = lax.dynamic_slice_in_dim(
        jnp.concatenate(
            [before, jnp.zeros(columns.shape[:-1] + (width - HD,), columns.dtype)], axis=-1
        ),
        0,
        width,
        axis=columns.ndim - 1,
    )
    return jnp.where(jnp.arange(width) < shift, front, rest)


def contract(left, right, left_dim, right_dim):
    return lax.dot_general(
        left, right, (((left_dim,), (right_dim,)), ((), ())), preferred_element_type=F32
    )


def attention_kernel(heads, chunk, qkv_ref, mask_ref, out_ref, lse_ref):
    rows = qkv_ref.shape[0]
    wide = heads * HD
    for head in range(heads):
        low = head * HD
        key = qkv_ref[:, wide + low : wide + low + HD]
        value = qkv_ref[:, 2 * wide + low : 2 * wide + low + HD]
        for start in range(0, rows, chunk):
            part = pl.ds(start, chunk)
            query = qkv_ref[part, low : low + HD] * jnp.asarray(score_scale, BF)
            scores = contract(key, query, 1, 1) + mask_ref[:, part]
            peak = jnp.max(scores, axis=0, keepdims=True)
            weights = jnp.exp(scores - peak)
            mass = jnp.sum(weights, axis=0, keepdims=True)
            lse_ref[head : head + 1, part] = peak + jnp.log(mass)
            mixed = contract(value, weights.astype(BF), 0, 0) / mass
            out_ref[part, low : low + HD] = mixed.T.astype(BF)


def attention_forward(qkv, mask):
    rows, three = qkv.shape
    wide = three // 3
    heads = wide // HD
    return pl.pallas_call(
        functools.partial(attention_kernel, heads, 256),
        out_shape=(
            jax.ShapeDtypeStruct((rows, wide), BF),
            jax.ShapeDtypeStruct((heads, rows), F32),
        ),
        compiler_params=pltpu.CompilerParams(vmem_limit_bytes=40 * 1024 * 1024),
        cost_estimate=pl.CostEstimate(
            flops=4 * rows * rows * wide, bytes_accessed=8 * rows * wide, transcendentals=rows * rows * heads
        ),
    )(qkv, mask)


def attention_grad_kernel(heads, chunk, qkv_ref, up_ref, lse_ref, mask_ref, grad_ref, sum_ref):
    rows = qkv_ref.shape[0]
    wide = heads * HD
    for head in range(heads):
        low = head * HD
        key = qkv_ref[:, wide + low : wide + low + HD]
        value = qkv_ref[:, 2 * wide + low : 2 * wide + low + HD]
        key_grad = jnp.zeros((rows, HD), F32)
        value_grad = jnp.zeros((rows, HD), F32)
        query_sum = jnp.zeros((1, HD), F32)
        for start in range(0, rows, chunk):
            part = pl.ds(start, chunk)
            query = qkv_ref[part, low : low + HD] * jnp.asarray(score_scale, BF)
            up = up_ref[part, low : low + HD]
            scores = contract(key, query, 1, 1) + mask_ref[:, part]
            weights = jnp.exp(scores - lse_ref[head : head + 1, part])
            value_grad = value_grad + contract(weights.astype(BF), up, 1, 0)
            slope = contract(value, up, 1, 1)
            delta = jnp.sum(weights * slope, axis=0, keepdims=True)
            scores_grad = (weights * (slope - delta)).astype(BF)
            key_grad = key_grad + contract(scores_grad, query, 1, 0)
            query_grad = (contract(key, scores_grad, 0, 0) * score_scale).T.astype(BF)
            grad_ref[part, low : low + HD] = query_grad
            query_sum = query_sum + jnp.sum(query_grad.astype(F32), axis=0, keepdims=True)
        grad_ref[:, wide + low : wide + low + HD] = key_grad.astype(BF)
        grad_ref[:, 2 * wide + low : 2 * wide + low + HD] = value_grad.astype(BF)
        sum_ref[0:1, low : low + HD] = query_sum
        sum_ref[1:2, low : low + HD] = jnp.sum(value_grad, axis=0, keepdims=True)


def attention_backward(qkv, up, lse, mask):
    rows, three = qkv.shape
    wide = three // 3
    heads = wide // HD
    return pl.pallas_call(
        functools.partial(attention_grad_kernel, heads, 256),
        out_shape=(
            jax.ShapeDtypeStruct((rows, three), BF),
            jax.ShapeDtypeStruct((2, wide), F32),
        ),
        compiler_params=pltpu.CompilerParams(vmem_limit_bytes=40 * 1024 * 1024),
        cost_estimate=pl.CostEstimate(
            flops=10 * rows * rows * wide, bytes_accessed=16 * rows * wide, transcendentals=rows * rows * heads
        ),
    )(qkv, up, lse, mask)


def row_stats(stream):
    mean = jnp.mean(stream, axis=1, keepdims=True)
    scale = lax.rsqrt(jnp.mean(stream * stream, axis=1, keepdims=True) - mean * mean + epsilon)
    return mean, scale


def norm(stream, gain, offset):
    mean, scale = row_stats(stream)
    return (((stream - mean) * scale) * gain + offset).astype(BF)


def norm_backward(incoming, stream, gain):
    mean, scale = row_stats(stream)
    normed = (stream - mean) * scale
    scaled = incoming * gain
    outgoing = scale * (
        scaled
        - jnp.mean(scaled, axis=1, keepdims=True)
        - normed * jnp.mean(scaled * normed, axis=1, keepdims=True)
    )
    return outgoing, jnp.sum(incoming * normed, axis=0), jnp.sum(incoming, axis=0)


def matmul(left, right):
    return contract(left, right, 1, 0)


def gelu_both(inputs):
    inner = tanh_scale * (inputs + cubic_weight * inputs * inputs * inputs)
    tangent = jnp.tanh(inner)
    value = 0.5 * inputs * (1.0 + tangent)
    slope = 0.5 * (1.0 + tangent) + 0.5 * inputs * (1.0 - tangent * tangent) * tanh_scale * (
        1.0 + 3.0 * cubic_weight * inputs * inputs
    )
    return value.astype(BF), slope.astype(BF)


def on_device(
    block_input,
    out_cotangent,
    group_order,
    first_gain,
    first_bias,
    query_weight,
    key_weight,
    value_weight,
    query_bias,
    value_bias,
    out_weight,
    out_bias,
    second_gain,
    second_bias,
    up_weight,
    up_bias,
    down_weight,
    down_bias,
):
    section = lax.axis_index("section")
    col = lax.axis_index("col")
    cols = lax.axis_size("col")
    batches, width, rows = block_input.shape
    own = rows // cols
    mine = batches // 2
    per, wide = head_share()
    features = width * cols

    def halves(pack):
        half = pack.shape[0] // 2
        keep = lax.dynamic_slice_in_dim(pack, section * half, half, 0)
        send = lax.dynamic_slice_in_dim(pack, (1 - section) * half, half, 0)
        got = swap_section(send)
        return jnp.where(section == 0, keep, got), jnp.where(section == 0, got, keep)

    def gather_rows(half):
        return lax.all_gather(half, ("row", "section"), axis=0, tiled=True)

    heads_pack = align_heads(
        jnp.stack([query_weight[0], key_weight[0], value_weight[0], out_weight[0].T]), col
    )
    heads_pack = jnp.concatenate([heads_pack[i] for i in range(4)], axis=1)
    heads_halves = halves(heads_pack)
    wide_halves = halves(jnp.concatenate([up_weight[0], down_weight[0]], axis=1))
    hidden_width = up_weight.shape[2]

    small_wide = jnp.stack(
        [first_gain[0], first_bias[0], out_bias[0], second_gain[0], second_bias[0], down_bias[0]]
    )
    small_wide = xor_order(
        jnp.stack([small_wide] + [xor_step(small_wide, "col", j) for j in range(1, cols)]), col
    )
    small_wide = jnp.swapaxes(small_wide, 0, 1).reshape(6, features)
    small_heads = align_heads(jnp.stack([query_bias[0], value_bias[0]]), col).reshape(-1)
    small_own = jnp.concatenate([small_wide.reshape(-1), small_heads, up_bias[0]])
    small_other = swap_section(small_own)
    small_layers = (
        jnp.where(section == 0, small_own, small_other),
        jnp.where(section == 0, small_other, small_own),
    )

    def smalls_of(layer):
        flat = small_layers[layer]
        vectors = flat[: 6 * features].reshape(6, features)
        query_shift = flat[6 * features : 6 * features + wide]
        value_shift = flat[6 * features + wide : 6 * features + 2 * wide]
        qkv_shift = jnp.concatenate([query_shift, jnp.zeros((wide,), F32), value_shift])
        return vectors, qkv_shift, flat[6 * features + 2 * wide :]

    smalls = [smalls_of(0), smalls_of(1)]

    def gather_features(values):
        local = lax.dynamic_slice_in_dim(values, section * mine, mine, 0)
        stack = xor_order(
            jnp.stack([local] + [xor_step(local, "col", j) for j in range(1, cols)]), col
        )
        whole = []
        for batch in range(mine):
            plane = stack[:, batch].reshape(features, rows)
            whole.append(xor_order(plane.T.reshape(cols, own, features), col).reshape(rows, features))
        return whole

    inputs = gather_features(block_input)
    cotangents = gather_features(out_cotangent)

    blocks = group_order.shape[0]
    group_rows = L // blocks
    places = jnp.arange(rows, dtype=jnp.int32)
    places = ((places // own) ^ col) * own + places % own
    within = places % L
    match = (within // group_rows)[:, None] == jnp.arange(blocks, dtype=jnp.int32)[None, :]
    position = (
        jnp.sum(jnp.where(match, group_order[None, :], 0), axis=1) * group_rows
        + within % group_rows
    )
    sequence = places // L
    allowed = (sequence[:, None] == sequence[None, :]) & (position[:, None] <= position[None, :])
    mask = jnp.where(allowed, 0.0, -jnp.inf).astype(F32)

    weights = []
    saved = [[None] * mine, [None] * mine]
    streams = [item[:own].astype(F32) for item in inputs]
    finals = []
    for layer in range(2):
        vectors, qkv_shift, up_shift = smalls[layer]
        gain_one, bias_one, out_shift, gain_two, bias_two, down_shift = [vectors[i] for i in range(6)]
        heads_full = gather_rows(heads_halves[layer])
        wide_full = gather_rows(wide_halves[layer])
        qkv_full = heads_full[:, : 3 * wide]
        out_full = heads_full[:, 3 * wide :]
        up_full = wide_full[:, :hidden_width]
        down_full = wide_full[:, hidden_width:]
        weights.append((qkv_full, out_full, up_full, down_full))
        for batch in range(mine):
            stream = streams[batch]
            if layer == 0:
                inputs_one = norm(inputs[batch].astype(F32), gain_one, bias_one)
            else:
                inputs_one = gather_tokens(norm(stream, gain_one, bias_one))
            qkv = (matmul(inputs_one, qkv_full) + qkv_shift).astype(BF)
            attended, lse = attention_forward(qkv, mask)
            out_terms = scatter_terms(contract(attended, out_full, 1, 1).astype(BF))
            middle = stream + total(out_terms) + out_shift
            inputs_two = gather_tokens(norm(middle, gain_two, bias_two))
            hidden, slope = gelu_both(matmul(inputs_two, up_full) + up_shift)
            if layer == 0:
                down_terms = scatter_terms(contract(hidden, down_full, 1, 1).astype(BF))
                streams[batch] = middle + total(down_terms) + down_shift
            else:
                part = contract(down_full, hidden, 1, 1)
                base = (middle + down_shift).T
                part = jnp.concatenate([part[:, :own] + base, part[:, own:]], axis=1).astype(BF)
                part = part.reshape(features, cols, own)
                part = jnp.stack(
                    [
                        lax.dynamic_index_in_dim(part, col ^ t, 1, keepdims=False)
                        for t in range(cols)
                    ],
                    axis=1,
                ).reshape(cols, width, rows)
                terms = [
                    lax.dynamic_index_in_dim(part, col, 0, keepdims=False)
                ] + [
                    xor_step(
                        lax.dynamic_index_in_dim(part, col ^ j, 0, keepdims=False), "col", j
                    )
                    for j in range(1, cols)
                ]
                finals.append(total(terms))
            saved[layer][batch] = (
                stream, inputs_one, qkv, attended, lse, middle, inputs_two, hidden, slope,
            )

    def scatter_rows(grad):
        return lax.psum_scatter(grad, ("row", "section"), scatter_dimension=0, tiled=True)

    reduced = [None, None]
    wide_sums = [None, None]
    narrow_sums = [None, None]
    upstream_full = cotangents
    upstream_own = [item[:own].astype(F32) for item in cotangents]
    for layer in (1, 0):
        vectors = smalls[layer][0]
        gain_one, gain_two = vectors[0], vectors[3]
        qkv_full, out_full, up_full, down_full = weights[layer]
        halves_of = [[] for _ in range(4)]
        hidden_grads = []
        middle_grads = []
        qkv_grads = []
        sums = []
        head_sums = []
        up_sums = []
        next_own = []
        for batch in range(mine):
            stream, inputs_one, qkv, attended, lse, middle, inputs_two, hidden, slope = saved[
                layer
            ][batch]
            hidden_grad = matmul(upstream_full[batch], down_full) * slope.astype(F32)
            up_sums.append(jnp.sum(hidden_grad, axis=0))
            hidden_half = hidden_grad.astype(BF)
            hidden_grads.append(hidden_half)
            incoming = total(scatter_terms(contract(hidden_half, up_full, 1, 1).astype(BF)))
            middle_part, gain_two_grad, bias_two_grad = norm_backward(incoming, middle, gain_two)
            middle_grad = upstream_own[batch] + middle_part
            middle_full = gather_tokens(middle_grad.astype(BF))
            middle_grads.append(middle_full)
            attended_grad = matmul(middle_full, out_full).astype(BF)
            qkv_grad, head_sum = attention_backward(qkv, attended_grad, lse, mask)
            qkv_grads.append(qkv_grad)
            head_sums.append(head_sum.reshape(-1))
            incoming = total(scatter_terms(contract(qkv_grad, qkv_full, 1, 1).astype(BF)))
            stream_part, gain_one_grad, bias_one_grad = norm_backward(incoming, stream, gain_one)
            stream_grad = middle_grad + stream_part
            next_own.append(stream_grad)
            sums.append(
                jnp.stack(
                    [
                        gain_one_grad,
                        bias_one_grad,
                        jnp.sum(middle_grad, axis=0),
                        gain_two_grad,
                        bias_two_grad,
                        jnp.sum(upstream_own[batch], axis=0),
                    ]
                )
            )
        both = [[saved[layer][batch][i] for batch in range(mine)] for i in (1, 3, 6, 7)]
        join = lambda pieces: jnp.concatenate(pieces, axis=0)
        down_grad = contract(join(upstream_full), join(both[3]), 0, 0).astype(BF)
        up_grad = contract(join(both[2]), join(hidden_grads), 0, 0).astype(BF)
        out_grad = contract(join(middle_grads), join(both[1]), 0, 0).astype(BF)
        qkv_weight_grad = contract(join(both[0]), join(qkv_grads), 0, 0).astype(BF)
        reduced[layer] = (
            scatter_rows(down_grad),
            scatter_rows(up_grad),
            scatter_rows(jnp.concatenate([qkv_weight_grad, out_grad], axis=1)),
        )
        wide_sums[layer] = sum(sums[1:], sums[0])
        narrow_sums[layer] = jnp.concatenate(
            [sum(head_sums[1:], head_sums[0]), sum(up_sums[1:], up_sums[0])]
        )
        upstream_own = next_own
        if layer == 1:
            upstream_full = [gather_tokens(item.astype(BF)) for item in next_own]

    wide_both = jnp.stack(wide_sums).reshape(2, 6, cols, width)
    wide_here = lax.dynamic_index_in_dim(wide_both, col, 2, keepdims=False)
    for j in range(1, cols):
        wide_here = wide_here + xor_step(
            lax.dynamic_index_in_dim(wide_both, col ^ j, 2, keepdims=False), "col", j
        )
    small_sums = jnp.concatenate([wide_here.reshape(2, -1), jnp.stack(narrow_sums)], axis=1)
    small_own = lax.dynamic_index_in_dim(small_sums, section, 0, keepdims=False)
    small_own = small_own + swap_section(
        lax.dynamic_index_in_dim(small_sums, 1 - section, 0, keepdims=False)
    )
    step = 1
    while step < lax.axis_size("row"):
        small_own = small_own + xor_step(small_own, "row", step)
        step *= 2
    small_out = small_own[: 6 * width].reshape(6, width)
    head_out = unalign_heads(
        small_own[6 * width : 6 * width + 2 * wide].reshape(2, wide), width, col
    )
    up_bias_grad = small_own[6 * width + 2 * wide :]

    def settle(first, second):
        got = swap_section(jnp.where(section == 0, second, first))
        keep = jnp.where(section == 0, first, second)
        low = jnp.where(section == 0, keep, got)
        high = jnp.where(section == 0, got, keep)
        return jnp.concatenate([low, high], axis=0)

    down_out = settle(reduced[0][0], reduced[1][0]).astype(F32)
    up_out = settle(reduced[0][1], reduced[1][1]).astype(F32)
    heads_out = settle(reduced[0][2], reduced[1][2])
    heads_out = unalign_heads(
        jnp.stack([heads_out[:, i * wide : (i + 1) * wide] for i in range(4)]), width, col
    ).astype(F32)

    outputs = jnp.stack(finals)
    grads = jnp.stack(upstream_own).astype(BF)
    grads = lax.all_to_all(
        jnp.swapaxes(grads, 1, 2), "col", split_axis=1, concat_axis=2, tiled=True
    ).astype(F32)
    got = swap_section(jnp.where(section == 0, outputs, grads))
    keep = jnp.where(section == 0, grads, outputs)
    boundary = jnp.concatenate(
        [jnp.where(section == 0, keep, got), jnp.where(section == 0, got, keep)], axis=0
    )

    return (
        boundary[None],
        small_out[0][None],
        small_out[1][None],
        heads_out[0][None],
        heads_out[1][None],
        heads_out[2][None],
        head_out[0][None],
        head_out[1][None],
        heads_out[3].T[None],
        small_out[2][None],
        small_out[3][None],
        small_out[4][None],
        up_out[None],
        up_bias_grad[None],
        down_out[None],
        small_out[5][None],
    )


def solution(mesh):
    vector = P("section", "col")
    matrix = P("section", "row", "col")
    turned = P("section", "col", "row")
    plane = P(None, "col", "row")
    in_specs = (
        plane, plane, P(), vector, vector, matrix, matrix, matrix, vector, vector,
        turned, vector, vector, vector, matrix, vector, matrix, vector,
    )
    out_specs = (
        P("section", None, "col", "row"), vector, vector, matrix, matrix, matrix, vector, vector,
        turned, vector, vector, vector, matrix, vector, matrix, vector,
    )
    return jax.shard_map(
        on_device, mesh=mesh, in_specs=in_specs, out_specs=out_specs, check_vma=False
    )
```

```python
import functools
import math

import jax
import jax.numpy as jnp
from jax import lax
from jax.experimental import pallas as pl
from jax.experimental.pallas import tpu as pltpu
from jax.sharding import PartitionSpec as P

H = 25
HD = 64
L = 512
BF = jnp.bfloat16
F32 = jnp.float32

epsilon = 1e-05
tanh_scale = math.sqrt(2.0 / math.pi)
cubic_weight = 0.044715
score_scale = HD ** (-0.5)


def xor_step(value, axis, step):
    count = lax.axis_size(axis)
    return lax.ppermute(value, axis, [(i, i ^ step) for i in range(count)])


class Link:
    def move(self, parts):
        return [xor_step(part, "col", j + 1) for j, part in enumerate(parts)]

    def spread(self, rows):
        return [rows] + self.move([rows] * (lax.axis_size("col") - 1))

    def exchange(self, parts):
        return [parts[0]] + self.move(list(parts[1:]))


def after(values, *tokens):
    return lax.optimization_barrier((values, tokens))[0]


def swap_section(value):
    return xor_step(value, "section", 1)


def xor_order(stack, index):
    count = stack.shape[0]
    return jnp.stack(
        [lax.dynamic_index_in_dim(stack, index ^ t, 0, keepdims=False) for t in range(count)]
    )


def head_share():
    count = lax.axis_size("col")
    return H // count, (H // count + 1) * HD


def head_shift(col_index):
    count = lax.axis_size("col")
    return jnp.where(col_index == 0, 0, HD - (HD // count) * col_index)


def align_heads(columns, col_index):
    count = lax.axis_size("col")
    per, wide = head_share()
    lead = columns.shape[:-1]
    after = lax.ppermute(columns[..., :HD], "col", [(i + 1, i) for i in range(count - 1)])
    own = columns.shape[-1]
    pad = max(0, wide + HD - own - HD)
    extended = jnp.concatenate([columns, after, jnp.zeros(lead + (pad,), columns.dtype)], axis=-1)
    moved = lax.dynamic_slice_in_dim(
        extended, head_shift(col_index), wide, axis=extended.ndim - 1
    )
    limit = jnp.where(col_index == 0, wide, per * HD)
    return jnp.where(jnp.arange(wide) < limit, moved, jnp.zeros((), moved.dtype))


def unalign_heads(columns, width, col_index):
    count = lax.axis_size("col")
    per, wide = head_share()
    shift = head_shift(col_index)
    begin = width - shift
    padded = jnp.concatenate(
        [columns, jnp.zeros(columns.shape[:-1] + (HD,), columns.dtype)], axis=-1
    )
    tail = lax.dynamic_slice_in_dim(padded, begin, HD, axis=columns.ndim - 1)
    before = lax.ppermute(tail, "col", [(i, i + 1) for i in range(count - 1)])
    joined = jnp.concatenate([before, columns], axis=-1)
    rest = lax.dynamic_slice_in_dim(
        jnp.concatenate(
            [joined, jnp.zeros(columns.shape[:-1] + (HD,), columns.dtype)], axis=-1
        ),
        HD - shift,
        width,
        axis=columns.ndim - 1,
    )
    front = lax.dynamic_slice_in_dim(
        jnp.concatenate(
            [before, jnp.zeros(columns.shape[:-1] + (width - HD,), columns.dtype)], axis=-1
        ),
        0,
        width,
        axis=columns.ndim - 1,
    )
    return jnp.where(jnp.arange(width) < shift, front, rest)


def contract(left, right, left_dim, right_dim):
    return lax.dot_general(
        left, right, (((left_dim,), (right_dim,)), ((), ())), preferred_element_type=F32
    )


def call(kernel, outs, args, scratch=(), flops=0, exps=0, anywhere=()):
    nbytes = sum(math.prod(x.shape) * x.dtype.itemsize for x in list(args) + list(outs))
    return pl.pallas_call(
        kernel,
        out_shape=tuple(outs),
        in_specs=[
            pl.BlockSpec(memory_space=pl.ANY if i in anywhere else pltpu.VMEM)
            for i in range(len(args))
        ],
        out_specs=tuple(pl.BlockSpec(memory_space=pltpu.VMEM) for _ in outs),
        scratch_shapes=list(scratch),
        compiler_params=pltpu.CompilerParams(vmem_limit_bytes=44 * 1024 * 1024),
        cost_estimate=pl.CostEstimate(flops=int(flops * WEIGHT), bytes_accessed=0, transcendentals=0),
    )(*args)


def shape(dims, kind):
    return jax.ShapeDtypeStruct(dims, kind)


class Matrix:
    def __init__(self, array, first, stride, block, count):
        self.array, self.first, self.stride = array, first, stride
        self.block, self.count = block, count

    @property
    def dims(self):
        return (self.block * self.count, self.array.shape[1])

    def copies(self, source, target, sems):
        return [
            pltpu.make_async_copy(
                source.at[pl.ds(self.first + self.stride * i, self.block), :],
                target.at[pl.ds(self.block * i, self.block), :],
                sems.at[i],
            )
            for i in range(self.count)
        ]

    def scratch(self):
        return [pltpu.VMEM(self.dims, BF), pltpu.SemaphoreType.DMA((self.count,))]


def fetch(matrices, sources, held):
    waits = []
    for matrix, source, (target, sems) in zip(matrices, sources, held):
        copies = matrix.copies(source, target, sems)
        for copy in copies:
            copy.start()
        waits.append(copies)
    return waits


def finish(copies):
    for copy in copies:
        copy.wait()


def stack_pieces(pieces, whole):
    begin = 0
    for piece in pieces:
        whole[begin : begin + piece.shape[0], :] = piece[...]
        begin += piece.shape[0]


def store_parts(parts, begin, value):
    here = parts[0].shape[0]
    for i in range(value.shape[0] // here):
        parts[begin // here + i][...] = value[i * here : (i + 1) * here].astype(BF)


CHUNK = 256
WEIGHT = 4


def heads_forward(pieces, first, second, bias, mask, heads, parts):
    rows = mask.shape[0]
    features = pieces[0].shape[1]
    wide = heads * HD
    count = len(pieces)

    def kernel(*refs):
        piece_refs, refs = refs[:count], refs[count:]
        first_hbm, second_hbm, bias_ref, mask_ref, qkv_ref, out_ref, lse_ref = refs[:7]
        part_refs, refs = refs[7 : 7 + parts], refs[7 + parts :]
        whole, first_ref, first_sem, second_ref, second_sem = refs
        waits = fetch(
            (first, second),
            (first_hbm, second_hbm),
            ((first_ref, first_sem), (second_ref, second_sem)),
        )
        stack_pieces(piece_refs, whole)
        finish(waits[0])
        for begin in range(0, rows, CHUNK):
            some = slice(begin, begin + CHUNK)
            value = contract(whole[some, :], first_ref[...], 1, 0) + bias_ref[:, : 2 * wide]
            qkv_ref[some, : 2 * wide] = value.astype(BF)
        finish(waits[1])
        for begin in range(0, rows, CHUNK):
            some = slice(begin, begin + CHUNK)
            value = contract(whole[some, :], second_ref[:, :wide], 1, 0) + bias_ref[:, 2 * wide :]
            qkv_ref[some, 2 * wide :] = value.astype(BF)
        for head in range(heads):
            low = head * HD
            key = qkv_ref[:, wide + low : wide + low + HD]
            value = qkv_ref[:, 2 * wide + low : 2 * wide + low + HD]
            for begin in range(0, rows, CHUNK):
                part = pl.ds(begin, CHUNK)
                query = qkv_ref[part, low : low + HD] * jnp.asarray(score_scale, BF)
                scores = contract(key, query, 1, 1) + mask_ref[:, part]
                peak = jnp.max(scores, axis=0, keepdims=True)
                weights = jnp.exp(scores - peak)
                mass = jnp.sum(weights, axis=0, keepdims=True)
                lse_ref[head : head + 1, part] = peak + jnp.log(mass)
                mixed = contract(value, weights.astype(BF), 0, 0) / mass
                out_ref[part, low : low + HD] = mixed.T.astype(BF)
        for begin in range(0, rows, CHUNK):
            some = slice(begin, begin + CHUNK)
            store_parts(part_refs, begin, contract(out_ref[some, :], second_ref[:, wide:], 1, 1))

    here = rows // parts
    result = call(
        kernel,
        [shape((rows, 3 * wide), BF), shape((rows, wide), BF), shape((heads, rows), F32)]
        + [shape((here, features), BF)] * parts,
        list(pieces) + [first.array, second.array, bias, mask],
        [pltpu.VMEM((rows, features), BF)] + first.scratch() + second.scratch(),
        flops=8 * rows * features * wide + 16 * rows * rows * wide,
        exps=rows * rows * heads,
        anywhere=(count, count + 1),
    )
    return result[0], result[1], result[2], result[3:]


def heads_backward(pieces, first, second, qkv, lse, mask, heads, parts):
    rows = mask.shape[0]
    features = pieces[0].shape[1]
    wide = heads * HD
    count = len(pieces)

    def kernel(*refs):
        piece_refs, refs = refs[:count], refs[count:]
        first_hbm, second_hbm, qkv_ref, lse_ref, mask_ref, grad_ref, sum_ref = refs[:7]
        part_refs, refs = refs[7 : 7 + parts], refs[7 + parts :]
        whole, up_ref, first_ref, first_sem, second_ref, second_sem = refs
        waits = fetch(
            (second, first),
            (second_hbm, first_hbm),
            ((second_ref, second_sem), (first_ref, first_sem)),
        )
        stack_pieces(piece_refs, whole)
        finish(waits[0])
        for begin in range(0, rows, CHUNK):
            some = slice(begin, begin + CHUNK)
            up_ref[some, :] = contract(whole[some, :], second_ref[:, wide:], 1, 0).astype(BF)
        for head in range(heads):
            low = head * HD
            key = qkv_ref[:, wide + low : wide + low + HD]
            value = qkv_ref[:, 2 * wide + low : 2 * wide + low + HD]
            key_grad = jnp.zeros((rows, HD), F32)
            value_grad = jnp.zeros((rows, HD), F32)
            query_sum = jnp.zeros((1, HD), F32)
            for begin in range(0, rows, CHUNK):
                part = pl.ds(begin, CHUNK)
                query = qkv_ref[part, low : low + HD] * jnp.asarray(score_scale, BF)
                up = up_ref[part, low : low + HD]
                scores = contract(key, query, 1, 1) + mask_ref[:, part]
                weights = jnp.exp(scores - lse_ref[head : head + 1, part])
                value_grad = value_grad + contract(weights.astype(BF), up, 1, 0)
                slope = contract(value, up, 1, 1)
                delta = jnp.sum(weights * slope, axis=0, keepdims=True)
                scores_grad = (weights * (slope - delta)).astype(BF)
                key_grad = key_grad + contract(scores_grad, query, 1, 0)
                query_grad = (contract(key, scores_grad, 0, 0) * score_scale).T.astype(BF)
                grad_ref[part, low : low + HD] = query_grad
                query_sum = query_sum + jnp.sum(query_grad.astype(F32), axis=0, keepdims=True)
            grad_ref[:, wide + low : wide + low + HD] = key_grad.astype(BF)
            grad_ref[:, 2 * wide + low : 2 * wide + low + HD] = value_grad.astype(BF)
            sum_ref[0:1, low : low + HD] = query_sum
            sum_ref[1:2, low : low + HD] = jnp.sum(value_grad, axis=0, keepdims=True)
        finish(waits[1])
        for begin in range(0, rows, CHUNK):
            some = slice(begin, begin + CHUNK)
            value = contract(grad_ref[some, : 2 * wide], first_ref[...], 1, 1)
            value = value + contract(grad_ref[some, 2 * wide :], second_ref[:, :wide], 1, 1)
            store_parts(part_refs, begin, value)

    here = rows // parts
    result = call(
        kernel,
        [shape((rows, 3 * wide), BF), shape((2, wide), F32)]
        + [shape((here, features), BF)] * parts,
        list(pieces) + [first.array, second.array, qkv, lse, mask],
        [pltpu.VMEM((rows, features), BF), pltpu.VMEM((rows, wide), BF)]
        + first.scratch()
        + second.scratch(),
        flops=8 * rows * features * wide + 40 * rows * rows * wide,
        exps=rows * rows * heads,
        anywhere=(count, count + 1),
    )
    return result[0], result[1], result[2:]


def gelu_both(inputs):
    inner = tanh_scale * (inputs + cubic_weight * inputs * inputs * inputs)
    tangent = jnp.tanh(inner)
    value = 0.5 * inputs * (1.0 + tangent)
    slope = 0.5 * (1.0 + tangent) + 0.5 * inputs * (1.0 - tangent * tangent) * tanh_scale * (
        1.0 + 3.0 * cubic_weight * inputs * inputs
    )
    return value.astype(BF), slope.astype(BF)


def feed_forward(pieces, up, down, bias, parts):
    rows = sum(piece.shape[0] for piece in pieces)
    features = pieces[0].shape[1]
    hidden = up.dims[1]
    count = len(pieces)

    def kernel(*refs):
        piece_refs, refs = refs[:count], refs[count:]
        up_hbm, down_hbm, bias_ref, hidden_ref, slope_ref = refs[:5]
        part_refs, refs = refs[5 : 5 + parts], refs[5 + parts :]
        whole, up_ref, up_sem, down_ref, down_sem = refs
        waits = fetch(
            (up, down), (up_hbm, down_hbm), ((up_ref, up_sem), (down_ref, down_sem))
        )
        stack_pieces(piece_refs, whole)
        finish(waits[0])
        for begin in range(0, rows, CHUNK):
            some = slice(begin, begin + CHUNK)
            value, slope = gelu_both(contract(whole[some, :], up_ref[...], 1, 0) + bias_ref[...])
            hidden_ref[some, :] = value
            slope_ref[some, :] = slope
        finish(waits[1])
        for begin in range(0, rows, CHUNK):
            some = slice(begin, begin + CHUNK)
            store_parts(part_refs, begin, contract(hidden_ref[some, :], down_ref[...], 1, 1))

    here = rows // parts
    result = call(
        kernel,
        [shape((rows, hidden), BF)] * 2 + [shape((here, features), BF)] * parts,
        list(pieces) + [up.array, down.array, bias],
        [pltpu.VMEM((rows, features), BF)] + up.scratch() + down.scratch(),
        flops=4 * rows * features * hidden,
        exps=rows * hidden,
        anywhere=(count, count + 1),
    )
    return result[0], result[1], result[2:]


def feed_backward(pieces, up, down, slope, parts):
    rows = sum(piece.shape[0] for piece in pieces)
    features = pieces[0].shape[1]
    hidden = up.dims[1]
    count = len(pieces)

    def kernel(*refs):
        piece_refs, refs = refs[:count], refs[count:]
        up_hbm, down_hbm, slope_ref, grad_ref, sum_ref = refs[:5]
        part_refs, refs = refs[5 : 5 + parts], refs[5 + parts :]
        whole, up_ref, up_sem, down_ref, down_sem = refs
        waits = fetch(
            (down, up), (down_hbm, up_hbm), ((down_ref, down_sem), (up_ref, up_sem))
        )
        stack_pieces(piece_refs, whole)
        finish(waits[0])
        for begin in range(0, rows, CHUNK):
            some = slice(begin, begin + CHUNK)
            value = contract(whole[some, :], down_ref[...], 1, 0) * slope_ref[some, :].astype(F32)
            grad_ref[some, :] = value.astype(BF)
            add = jnp.sum(value, axis=0, keepdims=True)
            sum_ref[...] = add if begin == 0 else sum_ref[...] + add
        finish(waits[1])
        for begin in range(0, rows, CHUNK):
            some = slice(begin, begin + CHUNK)
            store_parts(part_refs, begin, contract(grad_ref[some, :], up_ref[...], 1, 1))

    here = rows // parts
    result = call(
        kernel,
        [shape((rows, hidden), BF), shape((1, hidden), F32)]
        + [shape((here, features), BF)] * parts,
        list(pieces) + [up.array, down.array, slope],
        [pltpu.VMEM((rows, features), BF)] + up.scratch() + down.scratch(),
        flops=4 * rows * features * hidden,
        anywhere=(count, count + 1),
    )
    return result[0], result[1], result[2:]


def weight_grad(jobs):
    args = []
    for lefts, rights in jobs:
        args += list(lefts) + list(rights)
    features = jobs[0][0][0].shape[1]
    rows = sum(right.shape[0] for right in jobs[0][1])
    widths = [rights[0].shape[1] for _, rights in jobs]
    chunk = features // 4

    def kernel(*refs):
        refs = list(refs)
        turned, joined = refs[-2], refs[-1]
        out_ref = refs[len(args)]
        at = 0
        column = 0
        for (lefts, rights), width in zip(jobs, widths):
            begin = 0
            for _ in lefts:
                left = refs[at]
                at += 1
                turned[:, begin : begin + left.shape[0]] = left[...].T
                begin += left.shape[0]
            begin = 0
            for _ in rights:
                right = refs[at]
                at += 1
                joined[begin : begin + right.shape[0], :width] = right[...]
                begin += right.shape[0]

            for i in range(4):
                some = slice(i * chunk, (i + 1) * chunk)
                value = contract(turned[some, :], joined[:, :width], 1, 0)
                out_ref[some, column : column + width] = value.astype(BF)
            column += width

    return call(
        kernel,
        [shape((features, sum(widths)), BF)],
        args,
        [pltpu.VMEM((features, rows), BF), pltpu.VMEM((rows, max(widths)), BF)],
        flops=2 * rows * features * sum(widths),
    )[0]


def row_stats(stream):
    mean = jnp.mean(stream, axis=1, keepdims=True)
    scale = lax.rsqrt(jnp.mean(stream * stream, axis=1, keepdims=True) - mean * mean + epsilon)
    return mean, scale


def norm(stream, gain, offset):
    mean, scale = row_stats(stream)
    return (((stream - mean) * scale) * gain + offset).astype(BF)


def sum_refs(refs):
    value = refs[0][...].astype(F32)
    for ref in refs[1:]:
        value = value + ref[...].astype(F32)
    return value


def turn_blocks(blocks, gain, offset):
    cols = len(blocks)
    width, rows = blocks[0].shape
    own = rows // cols
    normed = gain is not None
    vectors = [gain, offset] if normed else []

    def kernel(*refs):
        block_refs, refs = refs[:cols], refs[cols:]
        vector_refs, refs = refs[: len(vectors)], refs[len(vectors) :]
        out_ref, own_ref, held = refs[0], refs[1], refs[-1]
        whole = refs[2] if normed else out_ref
        here = lax.axis_index("col")
        for j in range(cols):
            held[j] = block_refs[j][...]
        for t in range(cols):
            plane = held[here ^ t].T
            for i in range(cols):
                start = pl.multiple_of((here ^ i) * own, own)
                whole[pl.ds(start, own), t * width : (t + 1) * width] = plane[
                    i * own : (i + 1) * own
                ]
        own_ref[...] = whole[:own, :].astype(F32)
        if normed:
            for begin in range(0, rows, own):
                some = slice(begin, begin + own)
                value = whole[some, :].astype(F32)
                out_ref[some, :] = norm(value, vector_refs[0][...], vector_refs[1][...])

    full = (rows, width * cols)
    scratch = [pltpu.VMEM(full, BF)] if normed else []
    return call(
        kernel,
        [shape(full, BF), shape((own, full[1]), F32)],
        list(blocks) + vectors,
        scratch + [pltpu.VMEM((cols, width, rows), BF)],
    )


def add_and_norm(terms, stream, shift, gain, offset):
    count = len(terms)

    def kernel(*refs):
        stream_ref, shift_ref, gain_ref, offset_ref, sum_ref, norm_ref = refs[count:]
        value = stream_ref[...] + sum_refs(refs[:count]) + shift_ref[...]
        sum_ref[...] = value
        norm_ref[...] = norm(value, gain_ref[...], offset_ref[...])

    return call(
        kernel,
        [shape(stream.shape, F32), shape(stream.shape, BF)],
        list(terms) + [stream, shift, gain, offset],
    )


def add_and_turn(terms, stream, shift):
    count = len(terms)

    def kernel(*refs):
        stream_ref, shift_ref, out_ref = refs[count:]
        value = stream_ref[...] + sum_refs(refs[:count]) + shift_ref[...]
        out_ref[...] = value.T.astype(BF)

    return call(kernel, [shape(stream.shape[::-1], BF)], list(terms) + [stream, shift])[0]


def norm_backward(terms, stream, base, gain, turn, weight):
    count = len(terms)

    def kernel(*refs):
        stream_ref, base_ref, gain_ref, out_ref, half_ref, sum_ref = refs[count:]
        incoming = sum_refs(refs[:count])
        value = stream_ref[...]
        mean, scale = row_stats(value)
        normed = (value - mean) * scale
        scaled = incoming * gain_ref[...]
        outgoing = base_ref[...] + scale * (
            scaled
            - jnp.mean(scaled, axis=1, keepdims=True)
            - normed * jnp.mean(scaled * normed, axis=1, keepdims=True)
        )
        out_ref[...] = outgoing
        half_ref[...] = outgoing.T.astype(BF) if turn else outgoing.astype(BF)
        sum_ref[0:1, :] = jnp.sum(incoming * normed, axis=0, keepdims=True)
        sum_ref[1:2, :] = jnp.sum(incoming, axis=0, keepdims=True)
        sum_ref[2:3, :] = jnp.sum(outgoing, axis=0, keepdims=True)

    dims = stream.shape
    return call(
        kernel,
        [shape(dims, F32), shape(dims[::-1] if turn else dims, BF), shape((3, dims[1]), F32)],
        list(terms) + [stream, base, gain],
        flops=weight,
    )


def on_device(
    block_input,
    out_cotangent,
    group_order,
    first_gain,
    first_bias,
    query_weight,
    key_weight,
    value_weight,
    query_bias,
    value_bias,
    out_weight,
    out_bias,
    second_gain,
    second_bias,
    up_weight,
    up_bias,
    down_weight,
    down_bias,
):
    section = lax.axis_index("section")
    col = lax.axis_index("col")
    cols = lax.axis_size("col")
    batches, width, rows = block_input.shape
    own = rows // cols
    mine = batches // 2
    per, wide = head_share()
    heads = wide // HD
    features = width * cols
    is_first = section == 0

    def pairs(one, two):
        keep = jnp.where(is_first, one, two)
        got = swap_section(jnp.where(is_first, two, one))
        return jnp.where(is_first, keep, got), jnp.where(is_first, got, keep)

    def gather_pair(own_part):
        full = lax.all_gather(own_part, ("row", "section"), axis=0, tiled=True)
        block = own_part.shape[0]
        count = full.shape[0] // (2 * block)
        if block % 16 == 0:
            return (
                Matrix(full, 0, 2 * block, block, count),
                Matrix(full, block, 2 * block, block, count),
            )
        full = full.reshape(count, 2, block, -1)
        one = full[:, 0].reshape(count * block, -1)
        two = full[:, 1].reshape(count * block, -1)
        return Matrix(one, 0, 0, count * block, 1), Matrix(two, 0, 0, count * block, 1)

    heads_pack = align_heads(
        jnp.stack([query_weight[0], key_weight[0], value_weight[0], out_weight[0].T]), col
    )
    heads_parts = pairs(
        jnp.concatenate([heads_pack[0], heads_pack[1]], axis=1),
        jnp.concatenate([heads_pack[2], heads_pack[3]], axis=1),
    )

    small_wide = jnp.stack(
        [first_gain[0], first_bias[0], out_bias[0], second_gain[0], second_bias[0], down_bias[0]]
    )
    small_wide = xor_order(
        jnp.stack([small_wide] + [xor_step(small_wide, "col", j) for j in range(1, cols)]), col
    )
    small_wide = jnp.swapaxes(small_wide, 0, 1).reshape(6, features)
    small_heads = align_heads(jnp.stack([query_bias[0], value_bias[0]]), col).reshape(-1)
    small_own = jnp.concatenate([small_wide.reshape(-1), small_heads, up_bias[0]])
    small_other = swap_section(small_own)
    small_layers = (
        jnp.where(is_first, small_own, small_other),
        jnp.where(is_first, small_other, small_own),
    )

    def smalls_of(layer):
        flat = small_layers[layer]
        vectors = flat[: 6 * features].reshape(6, features)
        query_shift = flat[6 * features : 6 * features + wide]
        value_shift = flat[6 * features + wide : 6 * features + 2 * wide]
        qkv_shift = jnp.concatenate([query_shift, jnp.zeros((wide,), F32), value_shift])
        vectors = [vectors[i : i + 1] for i in range(6)]
        return vectors, qkv_shift[None], flat[6 * features + 2 * wide :][None]

    smalls = [smalls_of(0), smalls_of(1)]

    link = Link()
    input_own = lax.dynamic_slice_in_dim(block_input, section * mine, mine, 0)
    cotangent_own = lax.dynamic_slice_in_dim(out_cotangent, section * mine, mine, 0)
    early = link.spread(input_own[0])
    late_own = jnp.concatenate([input_own[1:], cotangent_own], axis=0)
    late = link.spread(after(late_own, small_layers, early))

    wide_parts = pairs(*after((up_weight[0], down_weight[0]), early))

    blocks = group_order.shape[0]
    group_rows = L // blocks
    places = jnp.arange(rows, dtype=jnp.int32)
    places = ((places // own) ^ col) * own + places % own
    within = places % L
    match = (within // group_rows)[:, None] == jnp.arange(blocks, dtype=jnp.int32)[None, :]
    position = (
        jnp.sum(jnp.where(match, group_order[None, :], 0), axis=1) * group_rows
        + within % group_rows
    )
    sequence = places // L
    allowed = (sequence[:, None] == sequence[None, :]) & (position[:, None] <= position[None, :])
    mask = jnp.where(allowed, 0.0, -jnp.inf).astype(F32)

    everyone = range(mine)
    weights = [gather_pair(heads_parts[0]) + gather_pair(wide_parts[0])]
    weights.append(gather_pair(heads_parts[1]) + gather_pair(wide_parts[1]))
    saved = [[None] * mine, [None] * mine]
    turned_input = turn_blocks(early, smalls[0][0][0], smalls[0][0][1])
    streams = [turned_input[1]]
    pieces = [[turned_input[0]]]
    for layer in range(2):
        vectors, qkv_shift, up_shift = smalls[layer]
        gain_one, bias_one, out_shift, gain_two, bias_two, down_shift = vectors
        first, second, up, down = weights[layer]
        begun = []
        for batch in everyone:
            qkv, attended, lse, parts = heads_forward(
                pieces[batch], first, second, qkv_shift, mask, heads, cols
            )
            begun.append((qkv, attended, lse, link.exchange(parts)))
            if layer == 0 and batch == 0:
                late = after(late, lse)
                for i in range(1, mine):
                    turned_input = turn_blocks(
                        [item[i - 1] for item in late], smalls[0][0][0], smalls[0][0][1]
                    )
                    streams.append(turned_input[1])
                    pieces.append([turned_input[0]])
                cotangents = [
                    turn_blocks([item[mine - 1 + i] for item in late], None, None)
                    for i in range(mine)
                ]
        middles = []
        for batch in everyone:
            middle, normed = add_and_norm(
                begun[batch][3], streams[batch], out_shift, gain_two, bias_two
            )
            middles.append((middle, link.spread(normed)))
        terms = []
        for batch in everyone:
            middle, twos = middles[batch]
            hidden, slope, parts = feed_forward(twos, up, down, up_shift, cols)
            saved[layer][batch] = (
                streams[batch], pieces[batch], *begun[batch][:3], middle, twos, hidden, slope,
            )
            terms.append(link.exchange(parts))
        if layer == 0:
            streams, pieces = [], []
            for batch in everyone:
                stream, normed = add_and_norm(
                    terms[batch], middles[batch][0], down_shift, smalls[1][0][0], smalls[1][0][1]
                )
                streams.append(stream)
                pieces.append(link.spread(normed))
        else:
            last_terms = terms
            finals = [
                add_and_turn(terms[batch], middles[batch][0], down_shift) for batch in everyone
            ]

    def to_features(pair):
        blocks_out = jnp.stack([item.reshape(cols, width, own) for item in pair], axis=1)
        blocks_in = lax.all_to_all(blocks_out, "col", split_axis=0, concat_axis=0, tiled=True)
        return blocks_in.transpose(1, 2, 0, 3).reshape(len(pair), width, rows)

    def scatter_rows(grad):
        return lax.psum_scatter(grad, ("row", "section"), scatter_dimension=0, tiled=True)

    reduced = [None, None]
    wide_sums = [None, None]
    narrow_sums = [None, None]
    ups = [[item[0]] for item in cotangents]
    bases = [item[1] for item in cotangents]
    base_sum = sum(jnp.sum(base, axis=0, keepdims=True) for base in bases)
    results = []
    turned = []
    for layer in (1, 0):
        vectors = smalls[layer][0]
        gain_one, gain_two = vectors[0], vectors[3]
        first, second, up, down = weights[layer]
        mids = []
        hidden_grads = []
        qkv_grads = []
        sums = []
        head_sums = []
        up_sums = []
        next_bases = []
        next_ups = []
        down_job = (ups[0] + ups[1], [saved[layer][batch][7] for batch in everyone])
        if layer == 1:
            down_grad = weight_grad([down_job])
            down_sum = scatter_rows(down_grad)
        terms = []
        for batch in everyone:
            slope = saved[layer][batch][8]
            slope = after(slope, down_grad if layer == 1 else first_sum)
            if layer == 1 and batch == mine - 1:
                slope = after(slope, last_terms)
            hidden_grad, hidden_sum, parts = feed_backward(ups[batch], up, down, slope, cols)
            hidden_grads.append(hidden_grad)
            up_sums.append(hidden_sum[0])
            terms.append(link.exchange(parts))
        up_job = (saved[layer][0][6] + saved[layer][1][6], hidden_grads)
        if layer == 1:
            up_grad = weight_grad([up_job])
            up_sum = scatter_rows(up_grad)
        else:
            wide_grad = weight_grad([down_job, up_job])
            wide_sum = scatter_rows(wide_grad)
        middle_grads = []
        seconds = []
        for batch in everyone:
            middle = saved[layer][batch][5]
            if layer == 1:
                middle = after(middle, up_grad)
            middle_grad, half, second_sums = norm_backward(
                terms[batch], middle, bases[batch], gain_two, False, layer * 15000000000
            )
            middle_grads.append(middle_grad)
            seconds.append(second_sums)
            mids.append(link.spread(half))
        terms = []
        for batch in everyone:
            qkv, lse = saved[layer][batch][2], saved[layer][batch][4]
            if layer == 0:
                lse = after(lse, wide_grad, reduced[1][2])
            qkv_grad, head_sum, parts = heads_backward(
                mids[batch], first, second, qkv, lse, mask, heads, cols
            )
            qkv_grads.append(qkv_grad)
            head_sums.append(head_sum.reshape(-1))
            terms.append(link.exchange(parts))
        heads_grad = weight_grad(
            [
                (saved[layer][0][1] + saved[layer][1][1], qkv_grads),
                (mids[0] + mids[1], [saved[layer][batch][3] for batch in everyone]),
            ]
        )
        for batch in everyone:
            stream = after(saved[layer][batch][0], heads_grad)
            stream_grad, half, first_sums = norm_backward(
                terms[batch], stream, middle_grads[batch], gain_one, layer == 0, layer * 15000000000
            )
            second_sums = seconds[batch]
            next_bases.append(stream_grad)
            if layer == 1:
                next_ups.append(link.spread(half))
            else:
                turned.append(half)
            sums.append((first_sums, second_sums))
        if layer == 1:
            wide_sum = jnp.concatenate([down_sum, up_sum], axis=1)
        first_sum = (down_sum, up_sum) if layer == 1 else None
        if layer == 0:
            heads_grad = after(heads_grad, wide_sum, turned)
        reduced[layer] = (wide_sum, up_sum, scatter_rows(heads_grad))
        first_sums = sums[0][0] + sums[1][0]
        second_sums = sums[0][1] + sums[1][1]
        wide_sums[layer] = jnp.concatenate(
            [first_sums[:2], second_sums[2:3], second_sums[:2], base_sum], axis=0
        )
        base_sum = first_sums[2:3]
        narrow_sums[layer] = jnp.concatenate(
            [head_sums[0] + head_sums[1], up_sums[0] + up_sums[1]]
        )
        bases = next_bases
        ups = next_ups

    both = to_features(turned + finals)
    grads, outputs = both[:mine], both[mine:]

    wide_both = jnp.stack(wide_sums).reshape(2, 6, cols, width)
    wide_here = lax.dynamic_index_in_dim(wide_both, col, 2, keepdims=False)
    for j in range(1, cols):
        wide_here = wide_here + xor_step(
            lax.dynamic_index_in_dim(wide_both, col ^ j, 2, keepdims=False), "col", j
        )
    small_sums = jnp.concatenate([wide_here.reshape(2, -1), jnp.stack(narrow_sums)], axis=1)
    small_own = lax.dynamic_index_in_dim(small_sums, section, 0, keepdims=False)
    small_own = small_own + swap_section(
        lax.dynamic_index_in_dim(small_sums, 1 - section, 0, keepdims=False)
    )
    step = 1
    while step < lax.axis_size("row"):
        small_own = small_own + xor_step(small_own, "row", step)
        step *= 2
    small_out = small_own[: 6 * width].reshape(6, width)
    head_out = unalign_heads(
        small_own[6 * width : 6 * width + 2 * wide].reshape(2, wide), width, col
    )
    up_bias_grad = small_own[6 * width + 2 * wide :]

    def settle(first_half, second_half):
        got = swap_section(jnp.where(is_first, second_half, first_half))
        keep = jnp.where(is_first, first_half, second_half)
        low = jnp.where(is_first, keep, got)
        high = jnp.where(is_first, got, keep)
        return jnp.concatenate([low, high], axis=0)

    wide_out = settle(reduced[0][0], reduced[1][0])
    down_out = wide_out[:, : wide_out.shape[1] // 2].astype(F32)
    up_out = wide_out[:, wide_out.shape[1] // 2 :].astype(F32)
    heads_out = settle(reduced[0][2], reduced[1][2])
    heads_out = unalign_heads(
        jnp.stack([heads_out[:, i * wide : (i + 1) * wide] for i in range(4)]), width, col
    ).astype(F32)

    got = swap_section(jnp.where(is_first, outputs, grads))
    keep = jnp.where(is_first, grads, outputs)
    boundary = jnp.concatenate(
        [jnp.where(is_first, keep, got), jnp.where(is_first, got, keep)], axis=0
    ).astype(F32)

    return (
        boundary[None],
        small_out[0][None],
        small_out[1][None],
        heads_out[0][None],
        heads_out[1][None],
        heads_out[2][None],
        head_out[0][None],
        head_out[1][None],
        heads_out[3].T[None],
        small_out[2][None],
        small_out[3][None],
        small_out[4][None],
        up_out[None],
        up_bias_grad[None],
        down_out[None],
        small_out[5][None],
    )


def solution(mesh):
    vector = P("section", "col")
    matrix = P("section", "row", "col")
    turned = P("section", "col", "row")
    plane = P(None, "col", "row")
    in_specs = (
        plane, plane, P(), vector, vector, matrix, matrix, matrix, vector, vector,
        turned, vector, vector, vector, matrix, vector, matrix, vector,
    )
    out_specs = (
        P("section", None, "col", "row"), vector, vector, matrix, matrix, matrix, vector, vector,
        turned, vector, vector, vector, matrix, vector, matrix, vector,
    )
    return jax.shard_map(
        on_device, mesh=mesh, in_specs=in_specs, out_specs=out_specs, check_vma=False
    )
```

```python
import functools
import math

import jax
import jax.numpy as jnp
from jax import lax
from jax.experimental import pallas as pl
from jax.experimental.pallas import tpu as pltpu
from jax.sharding import PartitionSpec as P

H = 25
HD = 64
L = 512
BF = jnp.bfloat16
F32 = jnp.float32

epsilon = 1e-05
tanh_scale = math.sqrt(2.0 / math.pi)
cubic_weight = 0.044715
score_scale = HD ** (-0.5)


def xor_step(value, axis, step):
    count = lax.axis_size(axis)
    return lax.ppermute(value, axis, [(i, i ^ step) for i in range(count)])


class Link:
    def move(self, parts):
        return [xor_step(part, "col", j + 1) for j, part in enumerate(parts)]

    def spread(self, rows):
        return [rows] + self.move([rows] * (lax.axis_size("col") - 1))

    def exchange(self, parts):
        return [parts[0]] + self.move(list(parts[1:]))


def after(values, *tokens):
    return lax.optimization_barrier((values, tokens))[0]


def swap_section(value):
    return xor_step(value, "section", 1)


def xor_order(stack, index):
    count = stack.shape[0]
    return jnp.stack(
        [lax.dynamic_index_in_dim(stack, index ^ t, 0, keepdims=False) for t in range(count)]
    )


def head_share():
    count = lax.axis_size("col")
    return H // count, (H // count + 1) * HD


def head_shift(col_index):
    count = lax.axis_size("col")
    return jnp.where(col_index == 0, 0, HD - (HD // count) * col_index)


def next_column(value):
    count = lax.axis_size("col")
    return lax.ppermute(value, "col", [(i + 1, i) for i in range(count - 1)])


def next_column_across(value):
    count = lax.axis_size("col")
    pairs = [
        ((1 - s) * count + i + 1, s * count + i) for s in range(2) for i in range(count - 1)
    ]
    return lax.ppermute(value, ("section", "col"), pairs)


def join_heads(columns, following, col_index):
    per, wide = head_share()
    lead = columns.shape[:-1]
    pad = max(0, wide - columns.shape[-1])
    extended = jnp.concatenate(
        [columns, following, jnp.zeros(lead + (pad,), columns.dtype)], axis=-1
    )
    moved = lax.dynamic_slice_in_dim(
        extended, head_shift(col_index), wide, axis=extended.ndim - 1
    )
    limit = jnp.where(col_index == 0, wide, per * HD)
    return jnp.where(jnp.arange(wide) < limit, moved, jnp.zeros((), moved.dtype))


def align_heads(columns, col_index):
    return join_heads(columns, next_column(columns[..., :HD]), col_index)


def tail_columns(columns, width, col_index):
    begin = width - head_shift(col_index)
    padded = jnp.concatenate(
        [columns, jnp.zeros(columns.shape[:-1] + (HD,), columns.dtype)], axis=-1
    )
    return lax.dynamic_slice_in_dim(padded, begin, HD, axis=columns.ndim - 1)


def split_heads(columns, before, width, col_index):
    shift = head_shift(col_index)
    pad = jnp.zeros(columns.shape[:-1] + (HD,), columns.dtype)
    joined = jnp.concatenate([before, columns, pad], axis=-1)
    rest = lax.dynamic_slice_in_dim(joined, HD - shift, width, axis=columns.ndim - 1)
    fill = jnp.zeros(columns.shape[:-1] + (width - HD,), columns.dtype)
    front = jnp.concatenate([before, fill], axis=-1)
    return jnp.where(jnp.arange(width) < shift, front, rest)


def previous_column(value):
    count = lax.axis_size("col")
    return lax.ppermute(value, "col", [(i, i + 1) for i in range(count - 1)])


def previous_column_across(value):
    count = lax.axis_size("col")
    pairs = [
        ((1 - s) * count + i, s * count + i + 1) for s in range(2) for i in range(count - 1)
    ]
    return lax.ppermute(value, ("section", "col"), pairs)


def contract(left, right, left_dim, right_dim):
    return lax.dot_general(
        left, right, (((left_dim,), (right_dim,)), ((), ())), preferred_element_type=F32
    )


def call(kernel, outs, args, scratch=(), flops=0, exps=0, anywhere=()):
    nbytes = sum(math.prod(x.shape) * x.dtype.itemsize for x in list(args) + list(outs))
    return pl.pallas_call(
        kernel,
        out_shape=tuple(outs),
        in_specs=[
            pl.BlockSpec(memory_space=pl.ANY if i in anywhere else pltpu.VMEM)
            for i in range(len(args))
        ],
        out_specs=tuple(pl.BlockSpec(memory_space=pltpu.VMEM) for _ in outs),
        scratch_shapes=list(scratch),
        compiler_params=pltpu.CompilerParams(vmem_limit_bytes=44 * 1024 * 1024),
        cost_estimate=pl.CostEstimate(flops=int(flops * WEIGHT), bytes_accessed=0, transcendentals=0),
    )(*args)


def shape(dims, kind):
    return jax.ShapeDtypeStruct(dims, kind)


class Matrix:
    def __init__(self, array, runs):
        self.array, self.runs = array, runs

    @property
    def dims(self):
        return (sum(run[2] for run in self.runs), self.array.shape[1])

    def copies(self, source, target, sems):
        return [
            pltpu.make_async_copy(
                source.at[pl.ds(begin, size), :], target.at[pl.ds(to, size), :], sems.at[i]
            )
            for i, (begin, to, size) in enumerate(self.runs)
        ]

    def scratch(self):
        return [pltpu.VMEM(self.dims, BF), pltpu.SemaphoreType.DMA((len(self.runs),))]


def fetch(matrices, sources, held):
    waits = []
    for matrix, source, (target, sems) in zip(matrices, sources, held):
        copies = matrix.copies(source, target, sems)
        for copy in copies:
            copy.start()
        waits.append(copies)
    return waits


def finish(copies):
    for copy in copies:
        copy.wait()


def stack_pieces(pieces, whole):
    begin = 0
    for piece in pieces:
        whole[begin : begin + piece.shape[0], :] = piece[...]
        begin += piece.shape[0]


def store_parts(parts, begin, value):
    here = parts[0].shape[0]
    for i in range(value.shape[0] // here):
        parts[begin // here + i][...] = value[i * here : (i + 1) * here].astype(BF)


CHUNK = 256
WEIGHT = 4


def heads_forward(pieces, first, second, bias, mask, heads, parts):
    rows = mask.shape[0]
    features = pieces[0].shape[1]
    wide = heads * HD
    count = len(pieces)

    def kernel(*refs):
        piece_refs, refs = refs[:count], refs[count:]
        first_hbm, second_hbm, bias_ref, mask_ref, qkv_ref, out_ref, lse_ref = refs[:7]
        part_refs, refs = refs[7 : 7 + parts], refs[7 + parts :]
        whole, first_ref, first_sem, second_ref, second_sem = refs
        waits = fetch(
            (first, second),
            (first_hbm, second_hbm),
            ((first_ref, first_sem), (second_ref, second_sem)),
        )
        stack_pieces(piece_refs, whole)
        finish(waits[0])
        for begin in range(0, rows, CHUNK):
            some = slice(begin, begin + CHUNK)
            value = contract(whole[some, :], first_ref[...], 1, 0) + bias_ref[:, : 2 * wide]
            qkv_ref[some, : 2 * wide] = value.astype(BF)
        finish(waits[1])
        for begin in range(0, rows, CHUNK):
            some = slice(begin, begin + CHUNK)
            value = contract(whole[some, :], second_ref[:, :wide], 1, 0) + bias_ref[:, 2 * wide :]
            qkv_ref[some, 2 * wide :] = value.astype(BF)
        for head in range(heads):
            low = head * HD
            key = qkv_ref[:, wide + low : wide + low + HD]
            value = qkv_ref[:, 2 * wide + low : 2 * wide + low + HD]
            for begin in range(0, rows, CHUNK):
                part = pl.ds(begin, CHUNK)
                query = qkv_ref[part, low : low + HD] * jnp.asarray(score_scale, BF)
                scores = contract(key, query, 1, 1) + mask_ref[:, part]
                peak = jnp.max(scores, axis=0, keepdims=True)
                weights = jnp.exp(scores - peak)
                mass = jnp.sum(weights, axis=0, keepdims=True)
                lse_ref[head : head + 1, part] = peak + jnp.log(mass)
                mixed = contract(value, weights.astype(BF), 0, 0) / mass
                out_ref[part, low : low + HD] = mixed.T.astype(BF)
        for begin in range(0, rows, CHUNK):
            some = slice(begin, begin + CHUNK)
            store_parts(part_refs, begin, contract(out_ref[some, :], second_ref[:, wide:], 1, 1))

    here = rows // parts
    result = call(
        kernel,
        [shape((rows, 3 * wide), BF), shape((rows, wide), BF), shape((heads, rows), F32)]
        + [shape((here, features), BF)] * parts,
        list(pieces) + [first.array, second.array, bias, mask],
        [pltpu.VMEM((rows, features), BF)] + first.scratch() + second.scratch(),
        flops=8 * rows * features * wide + 16 * rows * rows * wide,
        exps=rows * rows * heads,
        anywhere=(count, count + 1),
    )
    return result[0], result[1], result[2], result[3:]


def heads_backward(pieces, first, second, qkv, lse, mask, heads, parts, weight):
    rows = mask.shape[0]
    features = pieces[0].shape[1]
    wide = heads * HD
    count = len(pieces)

    def kernel(*refs):
        piece_refs, refs = refs[:count], refs[count:]
        first_hbm, second_hbm, qkv_ref, lse_ref, mask_ref, grad_ref, sum_ref = refs[:7]
        part_refs, refs = refs[7 : 7 + parts], refs[7 + parts :]
        whole, up_ref, first_ref, first_sem, second_ref, second_sem = refs
        waits = fetch(
            (second, first),
            (second_hbm, first_hbm),
            ((second_ref, second_sem), (first_ref, first_sem)),
        )
        stack_pieces(piece_refs, whole)
        finish(waits[0])
        for begin in range(0, rows, CHUNK):
            some = slice(begin, begin + CHUNK)
            up_ref[some, :] = contract(whole[some, :], second_ref[:, wide:], 1, 0).astype(BF)
        for head in range(heads):
            low = head * HD
            key = qkv_ref[:, wide + low : wide + low + HD]
            value = qkv_ref[:, 2 * wide + low : 2 * wide + low + HD]
            key_grad = jnp.zeros((rows, HD), F32)
            value_grad = jnp.zeros((rows, HD), F32)
            query_sum = jnp.zeros((1, HD), F32)
            for begin in range(0, rows, CHUNK):
                part = pl.ds(begin, CHUNK)
                query = qkv_ref[part, low : low + HD] * jnp.asarray(score_scale, BF)
                up = up_ref[part, low : low + HD]
                scores = contract(key, query, 1, 1) + mask_ref[:, part]
                weights = jnp.exp(scores - lse_ref[head : head + 1, part])
                value_grad = value_grad + contract(weights.astype(BF), up, 1, 0)
                slope = contract(value, up, 1, 1)
                delta = jnp.sum(weights * slope, axis=0, keepdims=True)
                scores_grad = (weights * (slope - delta)).astype(BF)
                key_grad = key_grad + contract(scores_grad, query, 1, 0)
                query_grad = (contract(key, scores_grad, 0, 0) * score_scale).T.astype(BF)
                grad_ref[part, low : low + HD] = query_grad
                query_sum = query_sum + jnp.sum(query_grad.astype(F32), axis=0, keepdims=True)
            grad_ref[:, wide + low : wide + low + HD] = key_grad.astype(BF)
            grad_ref[:, 2 * wide + low : 2 * wide + low + HD] = value_grad.astype(BF)
            sum_ref[0:1, low : low + HD] = query_sum
            sum_ref[1:2, low : low + HD] = jnp.sum(value_grad, axis=0, keepdims=True)
        finish(waits[1])
        for begin in range(0, rows, CHUNK):
            some = slice(begin, begin + CHUNK)
            value = contract(grad_ref[some, : 2 * wide], first_ref[...], 1, 1)
            value = value + contract(grad_ref[some, 2 * wide :], second_ref[:, :wide], 1, 1)
            store_parts(part_refs, begin, value)

    here = rows // parts
    result = call(
        kernel,
        [shape((rows, 3 * wide), BF), shape((2, wide), F32)]
        + [shape((here, features), BF)] * parts,
        list(pieces) + [first.array, second.array, qkv, lse, mask],
        [pltpu.VMEM((rows, features), BF), pltpu.VMEM((rows, wide), BF)]
        + first.scratch()
        + second.scratch(),
        flops=8 * rows * features * wide + 40 * rows * rows * wide + weight,
        exps=rows * rows * heads,
        anywhere=(count, count + 1),
    )
    return result[0], result[1], result[2:]


def gelu_both(inputs):
    inner = tanh_scale * (inputs + cubic_weight * inputs * inputs * inputs)
    tangent = jnp.tanh(inner)
    value = 0.5 * inputs * (1.0 + tangent)
    slope = 0.5 * (1.0 + tangent) + 0.5 * inputs * (1.0 - tangent * tangent) * tanh_scale * (
        1.0 + 3.0 * cubic_weight * inputs * inputs
    )
    return value.astype(BF), slope.astype(BF)


def feed_up(pieces, up, bias):
    rows = sum(piece.shape[0] for piece in pieces)
    features = pieces[0].shape[1]
    hidden = up.dims[1]
    count = len(pieces)

    def kernel(*refs):
        piece_refs, refs = refs[:count], refs[count:]
        up_hbm, bias_ref, hidden_ref, slope_ref, whole, up_ref, up_sem = refs
        (wait,) = fetch((up,), (up_hbm,), ((up_ref, up_sem),))
        stack_pieces(piece_refs, whole)
        finish(wait)
        for begin in range(0, rows, CHUNK):
            some = slice(begin, begin + CHUNK)
            value, slope = gelu_both(contract(whole[some, :], up_ref[...], 1, 0) + bias_ref[...])
            hidden_ref[some, :] = value
            slope_ref[some, :] = slope

    return call(
        kernel,
        [shape((rows, hidden), BF)] * 2,
        list(pieces) + [up.array, bias],
        [pltpu.VMEM((rows, features), BF)] + up.scratch(),
        flops=2 * rows * features * hidden,
        anywhere=(count,),
    )


def feed_down(hidden, down, parts):
    rows, units = hidden.shape
    features = down.dims[0]

    def kernel(*refs):
        hidden_ref, down_hbm = refs[:2]
        part_refs, (down_ref, down_sem) = refs[2 : 2 + parts], refs[2 + parts :]
        (wait,) = fetch((down,), (down_hbm,), ((down_ref, down_sem),))
        finish(wait)
        for begin in range(0, rows, CHUNK):
            some = slice(begin, begin + CHUNK)
            store_parts(part_refs, begin, contract(hidden_ref[some, :], down_ref[...], 1, 1))

    return call(
        kernel,
        [shape((rows // parts, features), BF)] * parts,
        [hidden, down.array],
        down.scratch(),
        flops=2 * rows * features * units,
        anywhere=(1,),
    )


def feed_forward(pieces, up, down, bias, parts):
    rows = sum(piece.shape[0] for piece in pieces)
    features = pieces[0].shape[1]
    hidden = up.dims[1]
    count = len(pieces)

    def kernel(*refs):
        piece_refs, refs = refs[:count], refs[count:]
        up_hbm, down_hbm, bias_ref, hidden_ref, slope_ref = refs[:5]
        part_refs, refs = refs[5 : 5 + parts], refs[5 + parts :]
        whole, up_ref, up_sem, down_ref, down_sem = refs
        waits = fetch(
            (up, down), (up_hbm, down_hbm), ((up_ref, up_sem), (down_ref, down_sem))
        )
        stack_pieces(piece_refs, whole)
        finish(waits[0])
        for begin in range(0, rows, CHUNK):
            some = slice(begin, begin + CHUNK)
            value, slope = gelu_both(contract(whole[some, :], up_ref[...], 1, 0) + bias_ref[...])
            hidden_ref[some, :] = value
            slope_ref[some, :] = slope
        finish(waits[1])
        for begin in range(0, rows, CHUNK):
            some = slice(begin, begin + CHUNK)
            store_parts(part_refs, begin, contract(hidden_ref[some, :], down_ref[...], 1, 1))

    here = rows // parts
    result = call(
        kernel,
        [shape((rows, hidden), BF)] * 2 + [shape((here, features), BF)] * parts,
        list(pieces) + [up.array, down.array, bias],
        [pltpu.VMEM((rows, features), BF)] + up.scratch() + down.scratch(),
        flops=4 * rows * features * hidden,
        exps=rows * hidden,
        anywhere=(count, count + 1),
    )
    return result[0], result[1], result[2:]


def feed_backward(pieces, up, down, slope, parts):
    rows = sum(piece.shape[0] for piece in pieces)
    features = pieces[0].shape[1]
    hidden = up.dims[1]
    count = len(pieces)

    def kernel(*refs):
        piece_refs, refs = refs[:count], refs[count:]
        up_hbm, down_hbm, slope_ref, grad_ref, sum_ref = refs[:5]
        part_refs, refs = refs[5 : 5 + parts], refs[5 + parts :]
        whole, up_ref, up_sem, down_ref, down_sem = refs
        waits = fetch(
            (down, up), (down_hbm, up_hbm), ((down_ref, down_sem), (up_ref, up_sem))
        )
        stack_pieces(piece_refs, whole)
        finish(waits[0])
        for begin in range(0, rows, CHUNK):
            some = slice(begin, begin + CHUNK)
            value = contract(whole[some, :], down_ref[...], 1, 0) * slope_ref[some, :].astype(F32)
            grad_ref[some, :] = value.astype(BF)
            add = jnp.sum(value, axis=0, keepdims=True)
            sum_ref[...] = add if begin == 0 else sum_ref[...] + add
        finish(waits[1])
        for begin in range(0, rows, CHUNK):
            some = slice(begin, begin + CHUNK)
            store_parts(part_refs, begin, contract(grad_ref[some, :], up_ref[...], 1, 1))

    here = rows // parts
    result = call(
        kernel,
        [shape((rows, hidden), BF), shape((1, hidden), F32)]
        + [shape((here, features), BF)] * parts,
        list(pieces) + [up.array, down.array, slope],
        [pltpu.VMEM((rows, features), BF)] + up.scratch() + down.scratch(),
        flops=4 * rows * features * hidden,
        anywhere=(count, count + 1),
    )
    return result[0], result[1], result[2:]


def weight_grad(jobs):
    args = []
    for lefts, rights in jobs:
        args += list(lefts) + list(rights)
    features = jobs[0][0][0].shape[1]
    rows = sum(right.shape[0] for right in jobs[0][1])
    widths = [rights[0].shape[1] for _, rights in jobs]
    chunk = features // 4

    def kernel(*refs):
        refs = list(refs)
        turned, joined = refs[-2], refs[-1]
        out_ref = refs[len(args)]
        at = 0
        column = 0
        for (lefts, rights), width in zip(jobs, widths):
            begin = 0
            for _ in lefts:
                left = refs[at]
                at += 1
                turned[:, begin : begin + left.shape[0]] = left[...].T
                begin += left.shape[0]
            begin = 0
            for _ in rights:
                right = refs[at]
                at += 1
                joined[begin : begin + right.shape[0], :width] = right[...]
                begin += right.shape[0]

            for i in range(4):
                some = slice(i * chunk, (i + 1) * chunk)
                value = contract(turned[some, :], joined[:, :width], 1, 0)
                out_ref[some, column : column + width] = value.astype(BF)
            column += width

    return call(
        kernel,
        [shape((features, sum(widths)), BF)],
        args,
        [pltpu.VMEM((features, rows), BF), pltpu.VMEM((rows, max(widths)), BF)],
        flops=2 * rows * features * sum(widths),
    )[0]


def row_stats(stream):
    mean = jnp.mean(stream, axis=1, keepdims=True)
    scale = lax.rsqrt(jnp.mean(stream * stream, axis=1, keepdims=True) - mean * mean + epsilon)
    return mean, scale


def norm(stream, gain, offset):
    mean, scale = row_stats(stream)
    return (((stream - mean) * scale) * gain + offset).astype(BF)


def sum_refs(refs):
    value = refs[0][...].astype(F32)
    for ref in refs[1:]:
        value = value + ref[...].astype(F32)
    return value


def turn_blocks(blocks, gain, offset):
    cols = len(blocks)
    width, rows = blocks[0].shape
    own = rows // cols
    normed = gain is not None
    vectors = [gain, offset] if normed else []

    def kernel(*refs):
        block_refs, refs = refs[:cols], refs[cols:]
        vector_refs, refs = refs[: len(vectors)], refs[len(vectors) :]
        out_ref, own_ref, held = refs[0], refs[1], refs[-1]
        whole = refs[2] if normed else out_ref
        here = lax.axis_index("col")
        for j in range(cols):
            held[j] = block_refs[j][...]
        for t in range(cols):
            plane = held[here ^ t].T
            for i in range(cols):
                start = pl.multiple_of((here ^ i) * own, own)
                whole[pl.ds(start, own), t * width : (t + 1) * width] = plane[
                    i * own : (i + 1) * own
                ]
        own_ref[...] = whole[:own, :].astype(F32)
        if normed:
            for begin in range(0, rows, own):
                some = slice(begin, begin + own)
                value = whole[some, :].astype(F32)
                out_ref[some, :] = norm(value, vector_refs[0][...], vector_refs[1][...])

    full = (rows, width * cols)
    scratch = [pltpu.VMEM(full, BF)] if normed else []
    return call(
        kernel,
        [shape(full, BF), shape((own, full[1]), F32)],
        list(blocks) + vectors,
        scratch + [pltpu.VMEM((cols, width, rows), BF)],
    )


def add_and_norm(terms, stream, shift, gain, offset):
    count = len(terms)

    def kernel(*refs):
        stream_ref, shift_ref, gain_ref, offset_ref, sum_ref, norm_ref = refs[count:]
        value = stream_ref[...] + sum_refs(refs[:count]) + shift_ref[...]
        sum_ref[...] = value
        norm_ref[...] = norm(value, gain_ref[...], offset_ref[...])

    return call(
        kernel,
        [shape(stream.shape, F32), shape(stream.shape, BF)],
        list(terms) + [stream, shift, gain, offset],
    )


def add_and_turn(terms, stream, shift):
    count = len(terms)

    def kernel(*refs):
        stream_ref, shift_ref, out_ref = refs[count:]
        value = stream_ref[...] + sum_refs(refs[:count]) + shift_ref[...]
        out_ref[...] = value.T.astype(BF)

    return call(kernel, [shape(stream.shape[::-1], BF)], list(terms) + [stream, shift])[0]


def norm_backward(terms, stream, base, gain, turn, weight):
    count = len(terms)

    def kernel(*refs):
        stream_ref, base_ref, gain_ref, out_ref, half_ref, sum_ref = refs[count:]
        incoming = sum_refs(refs[:count])
        value = stream_ref[...]
        mean, scale = row_stats(value)
        normed = (value - mean) * scale
        scaled = incoming * gain_ref[...]
        outgoing = base_ref[...] + scale * (
            scaled
            - jnp.mean(scaled, axis=1, keepdims=True)
            - normed * jnp.mean(scaled * normed, axis=1, keepdims=True)
        )
        out_ref[...] = outgoing
        half_ref[...] = outgoing.T.astype(BF) if turn else outgoing.astype(BF)
        sum_ref[0:1, :] = jnp.sum(incoming * normed, axis=0, keepdims=True)
        sum_ref[1:2, :] = jnp.sum(incoming, axis=0, keepdims=True)
        sum_ref[2:3, :] = jnp.sum(outgoing, axis=0, keepdims=True)

    dims = stream.shape
    return call(
        kernel,
        [shape(dims, F32), shape(dims[::-1] if turn else dims, BF), shape((3, dims[1]), F32)],
        list(terms) + [stream, base, gain],
        flops=weight,
    )


def on_device(
    block_input,
    out_cotangent,
    group_order,
    first_gain,
    first_bias,
    query_weight,
    key_weight,
    value_weight,
    query_bias,
    value_bias,
    out_weight,
    out_bias,
    second_gain,
    second_bias,
    up_weight,
    up_bias,
    down_weight,
    down_bias,
):
    section = lax.axis_index("section")
    col = lax.axis_index("col")
    cols = lax.axis_size("col")
    batches, width, rows = block_input.shape
    own = rows // cols
    mine = batches // 2
    per, wide = head_share()
    heads = wide // HD
    features = width * cols
    is_first = section == 0

    def gather_block(own_part):
        full = lax.all_gather(own_part, ("row", "section"), axis=0, tiled=True)
        return full, own_part.shape[0], full.shape[0] // (2 * own_part.shape[0])

    def gather_pair(own_part):
        full, block, count = gather_block(own_part)
        if block % 16 == 0:
            return tuple(
                Matrix(full, [((2 * i + k) * block, i * block, block) for i in range(count)])
                for k in range(2)
            )
        full = full.reshape(count, 2, block, -1)
        both = [full[:, k].reshape(count * block, -1) for k in range(2)]
        return tuple(Matrix(one, [(0, 0, count * block)]) for one in both)

    pair_one = jnp.stack([query_weight[0], key_weight[0]])
    pair_two = jnp.stack([value_weight[0], out_weight[0].T])
    keep = jnp.where(is_first, pair_one, pair_two)
    send = jnp.where(is_first, pair_two, pair_one)
    got = swap_section(send)
    keep_after = next_column(keep[..., :HD])
    got_after = next_column_across(send[..., :HD])
    keep = join_heads(keep, keep_after, col)
    got = join_heads(got, got_after, col)
    heads_parts = [
        jnp.concatenate([item[0], item[1]], axis=1)
        for item in (jnp.where(is_first, keep, got), jnp.where(is_first, got, keep))
    ]
    def exchange_wide(up_own, down_own):
        keep = jnp.where(is_first, up_own, down_own)
        got = swap_section(jnp.where(is_first, down_own, up_own))
        return jnp.where(is_first, keep, got), jnp.where(is_first, got, keep)

    small_wide = jnp.stack(
        [first_gain[0], first_bias[0], out_bias[0], second_gain[0], second_bias[0], down_bias[0]]
    )
    small_wide = xor_order(
        jnp.stack([small_wide] + [xor_step(small_wide, "col", j) for j in range(1, cols)]), col
    )
    small_wide = jnp.swapaxes(small_wide, 0, 1).reshape(6, features)
    small_heads = align_heads(jnp.stack([query_bias[0], value_bias[0]]), col).reshape(-1)
    small_own = jnp.concatenate([small_wide.reshape(-1), small_heads, up_bias[0]])
    small_other = swap_section(small_own)
    small_layers = (
        jnp.where(is_first, small_own, small_other),
        jnp.where(is_first, small_other, small_own),
    )

    def smalls_of(layer):
        flat = small_layers[layer]
        vectors = flat[: 6 * features].reshape(6, features)
        query_shift = flat[6 * features : 6 * features + wide]
        value_shift = flat[6 * features + wide : 6 * features + 2 * wide]
        qkv_shift = jnp.concatenate([query_shift, jnp.zeros((wide,), F32), value_shift])
        vectors = [vectors[i : i + 1] for i in range(6)]
        return vectors, qkv_shift[None], flat[6 * features + 2 * wide :][None]

    smalls = [smalls_of(0), smalls_of(1)]

    link = Link()
    input_own = lax.dynamic_slice_in_dim(block_input, section * mine, mine, 0)
    cotangent_own = lax.dynamic_slice_in_dim(out_cotangent, section * mine, mine, 0)
    early = link.spread(input_own)
    late = link.spread(after(cotangent_own, early))
    wide_first, wide_second = exchange_wide(
        *after((up_weight[0], down_weight[0]), heads_parts, early, small_layers)
    )

    blocks = group_order.shape[0]
    group_rows = L // blocks
    places = jnp.arange(rows, dtype=jnp.int32)
    places = ((places // own) ^ col) * own + places % own
    within = places % L
    match = (within // group_rows)[:, None] == jnp.arange(blocks, dtype=jnp.int32)[None, :]
    position = (
        jnp.sum(jnp.where(match, group_order[None, :], 0), axis=1) * group_rows
        + within % group_rows
    )
    sequence = places // L
    allowed = (sequence[:, None] == sequence[None, :]) & (position[:, None] <= position[None, :])
    mask = jnp.where(allowed, 0.0, -jnp.inf).astype(F32)

    everyone = range(mine)
    weights = [gather_pair(heads_parts[0]) + gather_pair(wide_first)]
    weights.append(gather_pair(heads_parts[1]) + gather_pair(wide_second))
    saved = [[None] * mine, [None] * mine]
    turned_inputs = [
        turn_blocks([item[i] for item in early], smalls[0][0][0], smalls[0][0][1])
        for i in range(mine)
    ]
    streams = [item[1] for item in turned_inputs]
    pieces = [[item[0]] for item in turned_inputs]
    for layer in range(2):
        vectors, qkv_shift, up_shift = smalls[layer]
        gain_one, bias_one, out_shift, gain_two, bias_two, down_shift = vectors
        first, second, up, down = weights[layer]
        begun = []
        for batch in everyone:
            qkv, attended, lse, parts = heads_forward(
                pieces[batch], first, second, qkv_shift, mask, heads, cols
            )
            begun.append((qkv, attended, lse, link.exchange(parts)))
            if layer == 0 and batch == 0:
                streams = after(streams, late)
                cotangents = [
                    turn_blocks([item[i] for item in late], None, None) for i in range(mine)
                ]
        middles = []
        for batch in everyone:
            middle, normed = add_and_norm(
                begun[batch][3], streams[batch], out_shift, gain_two, bias_two
            )
            middles.append((middle, link.spread(normed)))
        terms = []
        for batch in everyone:
            middle, twos = middles[batch]
            if layer == 0:
                hidden, slope, parts = feed_forward(twos, up, down, up_shift, cols)
                terms.append(link.exchange(parts))
            else:
                hidden, slope = feed_up(twos, up, up_shift)
            saved[layer][batch] = (
                streams[batch], pieces[batch], *begun[batch][:3], middle, twos, hidden, slope,
            )
        if layer == 0:
            streams, pieces = [], []
            for batch in everyone:
                stream, normed = add_and_norm(
                    terms[batch], middles[batch][0], down_shift, smalls[1][0][0], smalls[1][0][1]
                )
                streams.append(stream)
                pieces.append(link.spread(normed))

    def to_features(pair):
        blocks_out = jnp.stack([item.reshape(cols, width, own) for item in pair], axis=1)
        blocks_in = lax.all_to_all(blocks_out, "col", split_axis=0, concat_axis=0, tiled=True)
        return blocks_in.transpose(1, 2, 0, 3).reshape(len(pair), width, rows)

    def scatter_rows(grad):
        return lax.psum_scatter(grad, ("row", "section"), scatter_dimension=0, tiled=True)

    reduced = [None, None]
    wide_sums = [None, None]
    narrow_sums = [None, None]
    ups = [[item[0]] for item in cotangents]
    bases = [item[1] for item in cotangents]
    base_sum = sum(jnp.sum(base, axis=0, keepdims=True) for base in bases)
    results = []
    turned = []
    for layer in (1, 0):
        vectors = smalls[layer][0]
        gain_one, gain_two = vectors[0], vectors[3]
        first, second, up, down = weights[layer]
        mids = []
        hidden_grads = []
        qkv_grads = []
        sums = []
        head_sums = []
        up_sums = []
        next_bases = []
        next_ups = []
        down_job = (ups[0] + ups[1], [saved[layer][batch][7] for batch in everyone])
        if layer == 1:
            down_grad = weight_grad([down_job])
            down_sum = scatter_rows(down_grad)
        terms = []
        for batch in everyone:
            slope = saved[layer][batch][8]
            slope = after(slope, down_grad if layer == 1 else first_sum)
            hidden_grad, hidden_sum, parts = feed_backward(ups[batch], up, down, slope, cols)
            hidden_grads.append(hidden_grad)
            up_sums.append(hidden_sum[0])
            terms.append(link.exchange(parts))
        up_job = (saved[layer][0][6] + saved[layer][1][6], hidden_grads)
        if layer == 1:
            up_grad = weight_grad([up_job])
            up_sum = scatter_rows(up_grad)
        else:
            wide_grad = weight_grad([down_job, up_job])
            wide_sum = scatter_rows(wide_grad)
        middle_grads = []
        seconds = []
        for batch in everyone:
            middle = saved[layer][batch][5]
            if layer == 1:
                middle = after(middle, up_grad)
            middle_grad, half, second_sums = norm_backward(
                terms[batch], middle, bases[batch], gain_two, False,
                layer * 15000000000 + (1 - layer) * 15000000000,
            )
            middle_grads.append(middle_grad)
            seconds.append(second_sums)
            mids.append(link.spread(half))
        terms = []
        for batch in everyone:
            qkv, lse = saved[layer][batch][2], saved[layer][batch][4]
            if layer == 0:
                lse = after(lse, wide_grad, reduced[1][2])
            qkv_grad, head_sum, parts = heads_backward(
                mids[batch], first, second, qkv, lse, mask, heads, cols,
                (1 - layer) * 15000000000,
            )
            qkv_grads.append(qkv_grad)
            head_sums.append(head_sum.reshape(-1))
            terms.append(link.exchange(parts))
        heads_grad = weight_grad(
            [
                (saved[layer][0][1] + saved[layer][1][1], qkv_grads),
                (mids[0] + mids[1], [saved[layer][batch][3] for batch in everyone]),
            ]
        )
        for batch in everyone:
            stream = after(saved[layer][batch][0], heads_grad)
            stream_grad, half, first_sums = norm_backward(
                terms[batch], stream, middle_grads[batch], gain_one, layer == 0, layer * 15000000000
            )
            second_sums = seconds[batch]
            next_bases.append(stream_grad)
            if layer == 1:
                next_ups.append(link.spread(half))
            else:
                turned.append(half)
            sums.append((first_sums, second_sums))
        if layer == 1:
            wide_sum = jnp.concatenate([down_sum, up_sum], axis=1)
        first_sum = (down_sum, up_sum) if layer == 1 else None
        if layer == 0:
            heads_grad = after(heads_grad, wide_sum, turned)
        reduced[layer] = (wide_sum, up_sum, scatter_rows(heads_grad))
        first_sums = sums[0][0] + sums[1][0]
        second_sums = sums[0][1] + sums[1][1]
        wide_sums[layer] = jnp.concatenate(
            [first_sums[:2], second_sums[2:3], second_sums[:2], base_sum], axis=0
        )
        base_sum = first_sums[2:3]
        narrow_sums[layer] = jnp.concatenate(
            [head_sums[0] + head_sums[1], up_sums[0] + up_sums[1]]
        )
        bases = next_bases
        ups = next_ups


    last_parts = [
        feed_down(after(saved[1][batch][7], turned), weights[1][3], cols) for batch in everyone
    ]
    finals = []
    for batch in everyone:
        terms = link.exchange(last_parts[batch])
        finals.append(add_and_turn(terms, saved[1][batch][5], smalls[1][0][5]))

    wide_sums = after(wide_sums, last_parts)
    wide_both = jnp.stack(wide_sums).reshape(2, 6, cols, width)
    wide_here = lax.dynamic_index_in_dim(wide_both, col, 2, keepdims=False)
    for j in range(1, cols):
        wide_here = wide_here + xor_step(
            lax.dynamic_index_in_dim(wide_both, col ^ j, 2, keepdims=False), "col", j
        )
    small_sums = jnp.concatenate([wide_here.reshape(2, -1), jnp.stack(narrow_sums)], axis=1)
    small_own = lax.dynamic_index_in_dim(small_sums, section, 0, keepdims=False)
    small_own = small_own + swap_section(
        lax.dynamic_index_in_dim(small_sums, 1 - section, 0, keepdims=False)
    )
    step = 1
    while step < lax.axis_size("row"):
        small_own = small_own + xor_step(small_own, "row", step)
        step *= 2
    small_out = small_own[: 6 * width].reshape(6, width)
    head_out = small_own[6 * width : 6 * width + 2 * wide].reshape(2, wide)
    head_out = split_heads(
        head_out, previous_column(tail_columns(head_out, width, col)), width, col
    )
    up_bias_grad = small_own[6 * width + 2 * wide :]

    def settle(first_half, second_half):
        got = swap_section(jnp.where(is_first, second_half, first_half))
        keep = jnp.where(is_first, first_half, second_half)
        low = jnp.where(is_first, keep, got)
        high = jnp.where(is_first, got, keep)
        return jnp.concatenate([low, high], axis=0)

    wide_out = settle(reduced[0][0], reduced[1][0])
    down_out = wide_out[:, : wide_out.shape[1] // 2].astype(F32)
    up_out = wide_out[:, wide_out.shape[1] // 2 :].astype(F32)

    def by_matrix(flat):
        return jnp.stack([flat[:, i * wide : (i + 1) * wide] for i in range(4)])

    keep = by_matrix(jnp.where(is_first, reduced[0][2], reduced[1][2]))
    send = by_matrix(jnp.where(is_first, reduced[1][2], reduced[0][2]))
    got = swap_section(send)
    keep_before = previous_column(tail_columns(keep, width, col))
    got_before = previous_column_across(tail_columns(send, width, col))
    keep = split_heads(keep, keep_before, width, col)
    got = split_heads(got, got_before, width, col)
    heads_out = jnp.concatenate(
        [jnp.where(is_first, keep, got), jnp.where(is_first, got, keep)], axis=1
    ).astype(F32)

    both = to_features(turned + finals)
    grads, outputs = both[:mine], both[mine:]
    got = swap_section(jnp.where(is_first, outputs, grads))
    keep = jnp.where(is_first, grads, outputs)
    boundary = jnp.concatenate(
        [jnp.where(is_first, keep, got), jnp.where(is_first, got, keep)], axis=0
    ).astype(F32)

    return (
        boundary[None],
        small_out[0][None],
        small_out[1][None],
        heads_out[0][None],
        heads_out[1][None],
        heads_out[2][None],
        head_out[0][None],
        head_out[1][None],
        heads_out[3].T[None],
        small_out[2][None],
        small_out[3][None],
        small_out[4][None],
        up_out[None],
        up_bias_grad[None],
        down_out[None],
        small_out[5][None],
    )


def solution(mesh):
    vector = P("section", "col")
    matrix = P("section", "row", "col")
    turned = P("section", "col", "row")
    plane = P(None, "col", "row")
    in_specs = (
        plane, plane, P(), vector, vector, matrix, matrix, matrix, vector, vector,
        turned, vector, vector, vector, matrix, vector, matrix, vector,
    )
    out_specs = (
        P("section", None, "col", "row"), vector, vector, matrix, matrix, matrix, vector, vector,
        turned, vector, vector, vector, matrix, vector, matrix, vector,
    )
    return jax.shard_map(
        on_device, mesh=mesh, in_specs=in_specs, out_specs=out_specs, check_vma=False
    )
```

```python
import functools
import math

import jax
import jax.numpy as jnp
from jax import lax
from jax.experimental import pallas as pl
from jax.experimental.pallas import tpu as pltpu
from jax.sharding import PartitionSpec as P

H = 25
HD = 64
L = 512
BF = jnp.bfloat16
F32 = jnp.float32

epsilon = 1e-05
tanh_scale = math.sqrt(2.0 / math.pi)
cubic_weight = 0.044715
score_scale = HD ** (-0.5)


def xor_step(value, axis, step):
    count = lax.axis_size(axis)
    return lax.ppermute(value, axis, [(i, i ^ step) for i in range(count)])


class Link:
    def move(self, parts):
        return [xor_step(part, "col", j + 1) for j, part in enumerate(parts)]

    def spread(self, rows, axis=0):
        count = lax.axis_size("col")
        if count != 4:
            return [rows] + self.move([rows] * (count - 1))
        half = rows.shape[axis] // 2
        one, two = xor_step(rows, "col", 1), xor_step(rows, "col", 2)
        low = xor_step(lax.slice_in_dim(two, 0, half, axis=axis), "col", 1)
        high = xor_step(lax.slice_in_dim(one, half, 2 * half, axis=axis), "col", 2)
        return [rows, one, two, low, high]

    def exchange(self, parts):
        return [parts[0]] + self.move(list(parts[1:]))


def after(values, *tokens):
    return lax.optimization_barrier((values, tokens))[0]


def swap_section(value):
    return xor_step(value, "section", 1)


def xor_order(stack, index):
    count = stack.shape[0]
    return jnp.stack(
        [lax.dynamic_index_in_dim(stack, index ^ t, 0, keepdims=False) for t in range(count)]
    )


def head_share():
    count = lax.axis_size("col")
    return H // count, (H // count + 1) * HD


def head_shift(col_index):
    count = lax.axis_size("col")
    return jnp.where(col_index == 0, 0, HD - (HD // count) * col_index)


def next_column(value):
    count = lax.axis_size("col")
    return lax.ppermute(value, "col", [(i + 1, i) for i in range(count - 1)])


def next_column_across(value):
    count = lax.axis_size("col")
    pairs = [
        ((1 - s) * count + i + 1, s * count + i) for s in range(2) for i in range(count - 1)
    ]
    return lax.ppermute(value, ("section", "col"), pairs)


def join_heads(columns, following, col_index):
    per, wide = head_share()
    lead = columns.shape[:-1]
    pad = max(0, wide - columns.shape[-1])
    extended = jnp.concatenate(
        [columns, following, jnp.zeros(lead + (pad,), columns.dtype)], axis=-1
    )
    moved = lax.dynamic_slice_in_dim(
        extended, head_shift(col_index), wide, axis=extended.ndim - 1
    )
    limit = jnp.where(col_index == 0, wide, per * HD)
    return jnp.where(jnp.arange(wide) < limit, moved, jnp.zeros((), moved.dtype))


def align_heads(columns, col_index):
    return join_heads(columns, next_column(columns[..., :HD]), col_index)


def tail_columns(columns, width, col_index):
    begin = width - head_shift(col_index)
    padded = jnp.concatenate(
        [columns, jnp.zeros(columns.shape[:-1] + (HD,), columns.dtype)], axis=-1
    )
    return lax.dynamic_slice_in_dim(padded, begin, HD, axis=columns.ndim - 1)


def split_heads(columns, before, width, col_index):
    shift = head_shift(col_index)
    pad = jnp.zeros(columns.shape[:-1] + (HD,), columns.dtype)
    joined = jnp.concatenate([before, columns, pad], axis=-1)
    rest = lax.dynamic_slice_in_dim(joined, HD - shift, width, axis=columns.ndim - 1)
    fill = jnp.zeros(columns.shape[:-1] + (width - HD,), columns.dtype)
    front = jnp.concatenate([before, fill], axis=-1)
    return jnp.where(jnp.arange(width) < shift, front, rest)


def previous_column(value):
    count = lax.axis_size("col")
    return lax.ppermute(value, "col", [(i, i + 1) for i in range(count - 1)])


def previous_column_across(value):
    count = lax.axis_size("col")
    pairs = [
        ((1 - s) * count + i, s * count + i + 1) for s in range(2) for i in range(count - 1)
    ]
    return lax.ppermute(value, ("section", "col"), pairs)


def contract(left, right, left_dim, right_dim):
    return lax.dot_general(
        left, right, (((left_dim,), (right_dim,)), ((), ())), preferred_element_type=F32
    )


def call(kernel, outs, args, scratch=(), flops=0, exps=0, anywhere=()):
    nbytes = sum(math.prod(x.shape) * x.dtype.itemsize for x in list(args) + list(outs))
    return pl.pallas_call(
        kernel,
        out_shape=tuple(outs),
        in_specs=[
            pl.BlockSpec(memory_space=pl.ANY if i in anywhere else pltpu.VMEM)
            for i in range(len(args))
        ],
        out_specs=tuple(pl.BlockSpec(memory_space=pltpu.VMEM) for _ in outs),
        scratch_shapes=list(scratch),
        compiler_params=pltpu.CompilerParams(vmem_limit_bytes=44 * 1024 * 1024),
        cost_estimate=pl.CostEstimate(flops=int(flops * WEIGHT), bytes_accessed=0, transcendentals=0),
    )(*args)


def shape(dims, kind):
    return jax.ShapeDtypeStruct(dims, kind)


class Matrix:
    def __init__(self, array, runs):
        self.array, self.runs = array, runs

    @property
    def dims(self):
        return (sum(run[2] for run in self.runs), self.array.shape[1])

    def copies(self, source, target, sems):
        return [
            pltpu.make_async_copy(
                source.at[pl.ds(begin, size), :], target.at[pl.ds(to, size), :], sems.at[i]
            )
            for i, (begin, to, size) in enumerate(self.runs)
        ]

    def scratch(self):
        return [pltpu.VMEM(self.dims, BF), pltpu.SemaphoreType.DMA((len(self.runs),))]


def fetch(matrices, sources, held):
    waits = []
    for matrix, source, (target, sems) in zip(matrices, sources, held):
        copies = matrix.copies(source, target, sems)
        for copy in copies:
            copy.start()
        waits.append(copies)
    return waits


def finish(copies):
    for copy in copies:
        copy.wait()


def stack_pieces(pieces, whole):
    begin = 0
    for piece in pieces:
        whole[begin : begin + piece.shape[0], :] = piece[...]
        begin += piece.shape[0]


def store_parts(parts, begin, value):
    here = parts[0].shape[0]
    for i in range(value.shape[0] // here):
        parts[begin // here + i][...] = value[i * here : (i + 1) * here].astype(BF)


CHUNK = 256
WEIGHT = 4


def heads_forward(pieces, first, second, bias, mask, heads, parts):
    rows = mask.shape[0]
    features = pieces[0].shape[1]
    wide = heads * HD
    count = len(pieces)

    def kernel(*refs):
        piece_refs, refs = refs[:count], refs[count:]
        first_hbm, second_hbm, bias_ref, mask_ref, qkv_ref, out_ref, lse_ref = refs[:7]
        part_refs, refs = refs[7 : 7 + parts], refs[7 + parts :]
        whole, first_ref, first_sem, second_ref, second_sem = refs
        waits = fetch(
            (first, second),
            (first_hbm, second_hbm),
            ((first_ref, first_sem), (second_ref, second_sem)),
        )
        stack_pieces(piece_refs, whole)
        finish(waits[0])
        for begin in range(0, rows, CHUNK):
            some = slice(begin, begin + CHUNK)
            value = contract(whole[some, :], first_ref[...], 1, 0) + bias_ref[:, : 2 * wide]
            qkv_ref[some, : 2 * wide] = value.astype(BF)
        finish(waits[1])
        for begin in range(0, rows, CHUNK):
            some = slice(begin, begin + CHUNK)
            value = contract(whole[some, :], second_ref[:, :wide], 1, 0) + bias_ref[:, 2 * wide :]
            qkv_ref[some, 2 * wide :] = value.astype(BF)
        for head in range(heads):
            low = head * HD
            key = qkv_ref[:, wide + low : wide + low + HD]
            value = qkv_ref[:, 2 * wide + low : 2 * wide + low + HD]
            for begin in range(0, rows, CHUNK):
                part = pl.ds(begin, CHUNK)
                query = qkv_ref[part, low : low + HD] * jnp.asarray(score_scale, BF)
                scores = contract(key, query, 1, 1) + mask_ref[:, part]
                peak = jnp.max(scores, axis=0, keepdims=True)
                weights = jnp.exp(scores - peak)
                mass = jnp.sum(weights, axis=0, keepdims=True)
                lse_ref[head : head + 1, part] = peak + jnp.log(mass)
                mixed = contract(value, weights.astype(BF), 0, 0) / mass
                out_ref[part, low : low + HD] = mixed.T.astype(BF)
        for begin in range(0, rows, CHUNK):
            some = slice(begin, begin + CHUNK)
            store_parts(part_refs, begin, contract(out_ref[some, :], second_ref[:, wide:], 1, 1))

    here = rows // parts
    result = call(
        kernel,
        [shape((rows, 3 * wide), BF), shape((rows, wide), BF), shape((heads, rows), F32)]
        + [shape((here, features), BF)] * parts,
        list(pieces) + [first.array, second.array, bias, mask],
        [pltpu.VMEM((rows, features), BF)] + first.scratch() + second.scratch(),
        flops=8 * rows * features * wide + 16 * rows * rows * wide,
        exps=rows * rows * heads,
        anywhere=(count, count + 1),
    )
    return result[0], result[1], result[2], result[3:]


def heads_backward(pieces, first, second, qkv, lse, mask, heads, parts, weight):
    rows = mask.shape[0]
    features = pieces[0].shape[1]
    wide = heads * HD
    count = len(pieces)

    def kernel(*refs):
        piece_refs, refs = refs[:count], refs[count:]
        first_hbm, second_hbm, qkv_ref, lse_ref, mask_ref, grad_ref, sum_ref = refs[:7]
        part_refs, refs = refs[7 : 7 + parts], refs[7 + parts :]
        whole, up_ref, first_ref, first_sem, second_ref, second_sem = refs
        waits = fetch(
            (second, first),
            (second_hbm, first_hbm),
            ((second_ref, second_sem), (first_ref, first_sem)),
        )
        stack_pieces(piece_refs, whole)
        finish(waits[0])
        for begin in range(0, rows, CHUNK):
            some = slice(begin, begin + CHUNK)
            up_ref[some, :] = contract(whole[some, :], second_ref[:, wide:], 1, 0).astype(BF)
        for head in range(heads):
            low = head * HD
            key = qkv_ref[:, wide + low : wide + low + HD]
            value = qkv_ref[:, 2 * wide + low : 2 * wide + low + HD]
            key_grad = jnp.zeros((rows, HD), F32)
            value_grad = jnp.zeros((rows, HD), F32)
            query_sum = jnp.zeros((1, HD), F32)
            for begin in range(0, rows, CHUNK):
                part = pl.ds(begin, CHUNK)
                query = qkv_ref[part, low : low + HD] * jnp.asarray(score_scale, BF)
                up = up_ref[part, low : low + HD]
                scores = contract(key, query, 1, 1) + mask_ref[:, part]
                weights = jnp.exp(scores - lse_ref[head : head + 1, part])
                value_grad = value_grad + contract(weights.astype(BF), up, 1, 0)
                slope = contract(value, up, 1, 1)
                delta = jnp.sum(weights * slope, axis=0, keepdims=True)
                scores_grad = (weights * (slope - delta)).astype(BF)
                key_grad = key_grad + contract(scores_grad, query, 1, 0)
                query_grad = (contract(key, scores_grad, 0, 0) * score_scale).T.astype(BF)
                grad_ref[part, low : low + HD] = query_grad
                query_sum = query_sum + jnp.sum(query_grad.astype(F32), axis=0, keepdims=True)
            grad_ref[:, wide + low : wide + low + HD] = key_grad.astype(BF)
            grad_ref[:, 2 * wide + low : 2 * wide + low + HD] = value_grad.astype(BF)
            sum_ref[0:1, low : low + HD] = query_sum
            sum_ref[1:2, low : low + HD] = jnp.sum(value_grad, axis=0, keepdims=True)
        finish(waits[1])
        for begin in range(0, rows, CHUNK):
            some = slice(begin, begin + CHUNK)
            value = contract(grad_ref[some, : 2 * wide], first_ref[...], 1, 1)
            value = value + contract(grad_ref[some, 2 * wide :], second_ref[:, :wide], 1, 1)
            store_parts(part_refs, begin, value)

    here = rows // parts
    result = call(
        kernel,
        [shape((rows, 3 * wide), BF), shape((2, wide), F32)]
        + [shape((here, features), BF)] * parts,
        list(pieces) + [first.array, second.array, qkv, lse, mask],
        [pltpu.VMEM((rows, features), BF), pltpu.VMEM((rows, wide), BF)]
        + first.scratch()
        + second.scratch(),
        flops=8 * rows * features * wide + 40 * rows * rows * wide + weight,
        exps=rows * rows * heads,
        anywhere=(count, count + 1),
    )
    return result[0], result[1], result[2:]


def gelu_both(inputs):
    inner = tanh_scale * (inputs + cubic_weight * inputs * inputs * inputs)
    tangent = jnp.tanh(inner)
    value = 0.5 * inputs * (1.0 + tangent)
    slope = 0.5 * (1.0 + tangent) + 0.5 * inputs * (1.0 - tangent * tangent) * tanh_scale * (
        1.0 + 3.0 * cubic_weight * inputs * inputs
    )
    return value.astype(BF), slope.astype(BF)


def feed_up(pieces, up, bias):
    rows = sum(piece.shape[0] for piece in pieces)
    features = pieces[0].shape[1]
    hidden = up.dims[1]
    count = len(pieces)

    def kernel(*refs):
        piece_refs, refs = refs[:count], refs[count:]
        up_hbm, bias_ref, hidden_ref, slope_ref, whole, up_ref, up_sem = refs
        (wait,) = fetch((up,), (up_hbm,), ((up_ref, up_sem),))
        stack_pieces(piece_refs, whole)
        finish(wait)
        for begin in range(0, rows, CHUNK):
            some = slice(begin, begin + CHUNK)
            value, slope = gelu_both(contract(whole[some, :], up_ref[...], 1, 0) + bias_ref[...])
            hidden_ref[some, :] = value
            slope_ref[some, :] = slope

    return call(
        kernel,
        [shape((rows, hidden), BF)] * 2,
        list(pieces) + [up.array, bias],
        [pltpu.VMEM((rows, features), BF)] + up.scratch(),
        flops=2 * rows * features * hidden,
        anywhere=(count,),
    )


def feed_last(hiddens, middles, shift, down):
    rows, units = hiddens[0].shape
    own, features = middles[0].shape
    cols = rows // own
    width = features // cols
    count = len(hiddens)

    def kernel(*refs):
        hidden_refs, refs = refs[:count], refs[count:]
        middle_refs, refs = refs[:count], refs[count:]
        shift_ref, down_hbm = refs[:2]
        part_refs, refs = refs[2 : 2 + count * cols], refs[2 + count * cols :]
        ordered, whole, down_ref, down_sem = refs
        (wait,) = fetch((down,), (down_hbm,), ((down_ref, down_sem),))
        here = lax.axis_index("col")
        finish(wait)
        for i in range(count):
            for t in range(cols):
                start = pl.multiple_of((here ^ t) * own, own)
                ordered[t * own : (t + 1) * own, :] = hidden_refs[i][pl.ds(start, own), :]
            base = (middle_refs[i][...] + shift_ref[...]).T
            for begin in range(0, features, width):
                some = slice(begin, begin + width)
                value = contract(down_ref[some, :], ordered[...], 1, 1)
                for t in range(cols):
                    tokens = slice(t * own, (t + 1) * own)
                    extra = jnp.where(here == t, base[some, :], 0.0)
                    whole[some, tokens] = value[:, tokens] + extra
            for j in range(cols):
                start = pl.multiple_of((here ^ j) * width, 8)
                part_refs[i * cols + j][...] = whole[pl.ds(start, width), :].astype(BF)

    result = call(
        kernel,
        [shape((width, rows), BF)] * (count * cols),
        list(hiddens) + list(middles) + [shift, down.array],
        [pltpu.VMEM((rows, units), BF), pltpu.VMEM((features, rows), F32)] + down.scratch(),
        flops=2 * count * rows * features * units,
        anywhere=(2 * count + 1,),
    )
    return [result[i * cols : (i + 1) * cols] for i in range(count)]


def feed_forward(pieces, up, down, bias, parts):
    rows = sum(piece.shape[0] for piece in pieces)
    features = pieces[0].shape[1]
    hidden = up.dims[1]
    count = len(pieces)

    def kernel(*refs):
        piece_refs, refs = refs[:count], refs[count:]
        up_hbm, down_hbm, bias_ref, hidden_ref, slope_ref = refs[:5]
        part_refs, refs = refs[5 : 5 + parts], refs[5 + parts :]
        whole, up_ref, up_sem, down_ref, down_sem = refs
        waits = fetch(
            (up, down), (up_hbm, down_hbm), ((up_ref, up_sem), (down_ref, down_sem))
        )
        stack_pieces(piece_refs, whole)
        finish(waits[0])
        for begin in range(0, rows, CHUNK):
            some = slice(begin, begin + CHUNK)
            value, slope = gelu_both(contract(whole[some, :], up_ref[...], 1, 0) + bias_ref[...])
            hidden_ref[some, :] = value
            slope_ref[some, :] = slope
        finish(waits[1])
        for begin in range(0, rows, CHUNK):
            some = slice(begin, begin + CHUNK)
            store_parts(part_refs, begin, contract(hidden_ref[some, :], down_ref[...], 1, 1))

    here = rows // parts
    result = call(
        kernel,
        [shape((rows, hidden), BF)] * 2 + [shape((here, features), BF)] * parts,
        list(pieces) + [up.array, down.array, bias],
        [pltpu.VMEM((rows, features), BF)] + up.scratch() + down.scratch(),
        flops=4 * rows * features * hidden,
        exps=rows * hidden,
        anywhere=(count, count + 1),
    )
    return result[0], result[1], result[2:]


def feed_backward(pieces, up, down, slope, parts):
    rows = sum(piece.shape[0] for piece in pieces)
    features = pieces[0].shape[1]
    hidden = up.dims[1]
    count = len(pieces)

    def kernel(*refs):
        piece_refs, refs = refs[:count], refs[count:]
        up_hbm, down_hbm, slope_ref, grad_ref, sum_ref = refs[:5]
        part_refs, refs = refs[5 : 5 + parts], refs[5 + parts :]
        whole, up_ref, up_sem, down_ref, down_sem = refs
        waits = fetch(
            (down, up), (down_hbm, up_hbm), ((down_ref, down_sem), (up_ref, up_sem))
        )
        stack_pieces(piece_refs, whole)
        finish(waits[0])
        for begin in range(0, rows, CHUNK):
            some = slice(begin, begin + CHUNK)
            value = contract(whole[some, :], down_ref[...], 1, 0) * slope_ref[some, :].astype(F32)
            grad_ref[some, :] = value.astype(BF)
            add = jnp.sum(value, axis=0, keepdims=True)
            sum_ref[...] = add if begin == 0 else sum_ref[...] + add
        finish(waits[1])
        for begin in range(0, rows, CHUNK):
            some = slice(begin, begin + CHUNK)
            store_parts(part_refs, begin, contract(grad_ref[some, :], up_ref[...], 1, 1))

    here = rows // parts
    result = call(
        kernel,
        [shape((rows, hidden), BF), shape((1, hidden), F32)]
        + [shape((here, features), BF)] * parts,
        list(pieces) + [up.array, down.array, slope],
        [pltpu.VMEM((rows, features), BF)] + up.scratch() + down.scratch(),
        flops=4 * rows * features * hidden,
        anywhere=(count, count + 1),
    )
    return result[0], result[1], result[2:]


def weight_grad(jobs):
    args = []
    for lefts, rights in jobs:
        args += list(lefts) + list(rights)
    features = jobs[0][0][0].shape[1]
    rows = sum(right.shape[0] for right in jobs[0][1])
    widths = [rights[0].shape[1] for _, rights in jobs]
    chunk = features // 4

    def kernel(*refs):
        refs = list(refs)
        turned, joined = refs[-2], refs[-1]
        out_ref = refs[len(args)]
        at = 0
        column = 0
        for (lefts, rights), width in zip(jobs, widths):
            begin = 0
            for _ in lefts:
                left = refs[at]
                at += 1
                turned[:, begin : begin + left.shape[0]] = left[...].T
                begin += left.shape[0]
            begin = 0
            for _ in rights:
                right = refs[at]
                at += 1
                joined[begin : begin + right.shape[0], :width] = right[...]
                begin += right.shape[0]

            for i in range(4):
                some = slice(i * chunk, (i + 1) * chunk)
                value = contract(turned[some, :], joined[:, :width], 1, 0)
                out_ref[some, column : column + width] = value.astype(BF)
            column += width

    return call(
        kernel,
        [shape((features, sum(widths)), BF)],
        args,
        [pltpu.VMEM((features, rows), BF), pltpu.VMEM((rows, max(widths)), BF)],
        flops=2 * rows * features * sum(widths),
    )[0]


def row_stats(stream):
    mean = jnp.mean(stream, axis=1, keepdims=True)
    scale = lax.rsqrt(jnp.mean(stream * stream, axis=1, keepdims=True) - mean * mean + epsilon)
    return mean, scale


def norm(stream, gain, offset):
    mean, scale = row_stats(stream)
    return (((stream - mean) * scale) * gain + offset).astype(BF)


def sum_refs(refs):
    value = refs[0][...].astype(F32)
    for ref in refs[1:]:
        value = value + ref[...].astype(F32)
    return value


def turn_blocks(blocks, gain, offset):
    count = len(blocks)
    width, rows = blocks[0].shape
    cols = lax.axis_size("col")
    own = rows // cols
    normed = gain is not None
    vectors = [gain, offset] if normed else []

    def kernel(*refs):
        block_refs, refs = refs[:count], refs[count:]
        vector_refs, refs = refs[: len(vectors)], refs[len(vectors) :]
        out_ref, own_ref, held = refs[0], refs[1], refs[-1]
        whole = refs[2] if normed else out_ref
        here = lax.axis_index("col")
        at = 0
        for block_ref in block_refs:
            columns = block_ref.shape[1]
            held[at // rows, :, at % rows : at % rows + columns] = block_ref[...]
            at += columns
        for t in range(cols):
            plane = held[here ^ t].T
            for i in range(cols):
                start = pl.multiple_of((here ^ i) * own, own)
                whole[pl.ds(start, own), t * width : (t + 1) * width] = plane[
                    i * own : (i + 1) * own
                ]
        own_ref[...] = whole[:own, :].astype(F32)
        if normed:
            for begin in range(0, rows, own):
                some = slice(begin, begin + own)
                value = whole[some, :].astype(F32)
                out_ref[some, :] = norm(value, vector_refs[0][...], vector_refs[1][...])

    full = (rows, width * cols)
    scratch = [pltpu.VMEM(full, BF)] if normed else []
    return call(
        kernel,
        [shape(full, BF), shape((own, full[1]), F32)],
        list(blocks) + vectors,
        scratch + [pltpu.VMEM((cols, width, rows), BF)],
    )


def add_and_norm(terms, stream, shift, gain, offset):
    count = len(terms)

    def kernel(*refs):
        stream_ref, shift_ref, gain_ref, offset_ref, sum_ref, norm_ref = refs[count:]
        value = stream_ref[...] + sum_refs(refs[:count]) + shift_ref[...]
        sum_ref[...] = value
        norm_ref[...] = norm(value, gain_ref[...], offset_ref[...])

    return call(
        kernel,
        [shape(stream.shape, F32), shape(stream.shape, BF)],
        list(terms) + [stream, shift, gain, offset],
    )


def norm_backward(terms, stream, base, gain, turn, weight):
    count = len(terms)

    def kernel(*refs):
        stream_ref, base_ref, gain_ref, out_ref, half_ref, sum_ref = refs[count:]
        incoming = sum_refs(refs[:count])
        value = stream_ref[...]
        mean, scale = row_stats(value)
        normed = (value - mean) * scale
        scaled = incoming * gain_ref[...]
        outgoing = base_ref[...] + scale * (
            scaled
            - jnp.mean(scaled, axis=1, keepdims=True)
            - normed * jnp.mean(scaled * normed, axis=1, keepdims=True)
        )
        out_ref[...] = outgoing
        half_ref[...] = outgoing.T.astype(BF) if turn else outgoing.astype(BF)
        sum_ref[0:1, :] = jnp.sum(incoming * normed, axis=0, keepdims=True)
        sum_ref[1:2, :] = jnp.sum(incoming, axis=0, keepdims=True)
        sum_ref[2:3, :] = jnp.sum(outgoing, axis=0, keepdims=True)

    dims = stream.shape
    return call(
        kernel,
        [shape(dims, F32), shape(dims[::-1] if turn else dims, BF), shape((3, dims[1]), F32)],
        list(terms) + [stream, base, gain],
        flops=weight,
    )


def on_device(
    block_input,
    out_cotangent,
    group_order,
    first_gain,
    first_bias,
    query_weight,
    key_weight,
    value_weight,
    query_bias,
    value_bias,
    out_weight,
    out_bias,
    second_gain,
    second_bias,
    up_weight,
    up_bias,
    down_weight,
    down_bias,
):
    section = lax.axis_index("section")
    col = lax.axis_index("col")
    cols = lax.axis_size("col")
    batches, width, rows = block_input.shape
    own = rows // cols
    mine = batches // 2
    per, wide = head_share()
    heads = wide // HD
    features = width * cols
    is_first = section == 0

    def gather_block(own_part):
        full = lax.all_gather(own_part, ("row", "section"), axis=0, tiled=True)
        return full, own_part.shape[0], full.shape[0] // (2 * own_part.shape[0])

    def gather_pair(own_part):
        full, block, count = gather_block(own_part)
        if block % 16 == 0:
            return tuple(
                Matrix(full, [((2 * i + k) * block, i * block, block) for i in range(count)])
                for k in range(2)
            )
        full = full.reshape(count, 2, block, -1)
        both = [full[:, k].reshape(count * block, -1) for k in range(2)]
        return tuple(Matrix(one, [(0, 0, count * block)]) for one in both)

    def gather_halves(own_part, block):
        full, low, count = gather_block(own_part)
        high = block - low
        if low % 16 == 0 and high % 16 == 0:
            runs = []
            for i in range(count):
                runs.append((2 * i * low, i * block, low))
                runs.append(((2 * i + 1) * low, i * block + low, high))
            return Matrix(full, runs)
        full = full.reshape(count, 2 * low, -1)[:, :block].reshape(count * block, -1)
        return Matrix(full, [(0, 0, count * block)])

    pair_one = jnp.stack([query_weight[0], key_weight[0]])
    pair_two = jnp.stack([value_weight[0], out_weight[0].T])
    keep = jnp.where(is_first, pair_one, pair_two)
    send = jnp.where(is_first, pair_two, pair_one)
    got = swap_section(send)
    keep_after = next_column(keep[..., :HD])
    got_after = next_column_across(send[..., :HD])
    keep = join_heads(keep, keep_after, col)
    got = join_heads(got, got_after, col)
    heads_parts = [
        jnp.concatenate([item[0], item[1]], axis=1)
        for item in (jnp.where(is_first, keep, got), jnp.where(is_first, got, keep))
    ]
    block = up_weight.shape[1]
    low = block // 2
    low += -low % 16 if block % 16 == 0 else 0

    def exchange_wide(up_own, down_own):
        fill = jnp.zeros((2 * low - block, up_own.shape[1]), BF)
        lows = jnp.concatenate([up_own[:low], down_own[:low]])
        got = swap_section(jnp.where(is_first, jnp.concatenate([down_own, fill]), lows))
        first_layer = jnp.where(is_first, up_own, got[:block])
        seconds = [
            jnp.where(is_first, got[begin : begin + low], jnp.concatenate([item[low:], fill]))
            for begin, item in ((0, up_own), (low, down_own))
        ]
        return first_layer, seconds

    small_wide = jnp.stack(
        [first_gain[0], first_bias[0], out_bias[0], second_gain[0], second_bias[0], down_bias[0]]
    )
    small_wide = xor_order(
        jnp.stack([small_wide] + [xor_step(small_wide, "col", j) for j in range(1, cols)]), col
    )
    small_wide = jnp.swapaxes(small_wide, 0, 1).reshape(6, features)
    small_heads = align_heads(jnp.stack([query_bias[0], value_bias[0]]), col).reshape(-1)
    small_own = jnp.concatenate([small_wide.reshape(-1), small_heads, up_bias[0]])
    small_other = swap_section(small_own)
    small_layers = (
        jnp.where(is_first, small_own, small_other),
        jnp.where(is_first, small_other, small_own),
    )

    def smalls_of(layer):
        flat = small_layers[layer]
        vectors = flat[: 6 * features].reshape(6, features)
        query_shift = flat[6 * features : 6 * features + wide]
        value_shift = flat[6 * features + wide : 6 * features + 2 * wide]
        qkv_shift = jnp.concatenate([query_shift, jnp.zeros((wide,), F32), value_shift])
        vectors = [vectors[i : i + 1] for i in range(6)]
        return vectors, qkv_shift[None], flat[6 * features + 2 * wide :][None]

    smalls = [smalls_of(0), smalls_of(1)]

    link = Link()
    input_own = lax.dynamic_slice_in_dim(block_input, section * mine, mine, 0)
    cotangent_own = lax.dynamic_slice_in_dim(out_cotangent, section * mine, mine, 0)
    early = link.spread(input_own, 2)
    late = link.spread(after(cotangent_own, early), 2)
    wide_first, wide_second = exchange_wide(
        *after((up_weight[0], down_weight[0]), heads_parts, early, small_layers)
    )

    blocks = group_order.shape[0]
    group_rows = L // blocks
    places = jnp.arange(rows, dtype=jnp.int32)
    places = ((places // own) ^ col) * own + places % own
    within = places % L
    match = (within // group_rows)[:, None] == jnp.arange(blocks, dtype=jnp.int32)[None, :]
    position = (
        jnp.sum(jnp.where(match, group_order[None, :], 0), axis=1) * group_rows
        + within % group_rows
    )
    sequence = places // L
    allowed = (sequence[:, None] == sequence[None, :]) & (position[:, None] <= position[None, :])
    mask = jnp.where(allowed, 0.0, -jnp.inf).astype(F32)

    everyone = range(mine)
    weights = [gather_pair(heads_parts[0]) + gather_pair(wide_first)]
    weights.append(
        gather_pair(heads_parts[1])
        + tuple(gather_halves(item, block) for item in wide_second)
    )
    saved = [[None] * mine, [None] * mine]
    turned_inputs = [
        turn_blocks([item[i] for item in early], smalls[0][0][0], smalls[0][0][1])
        for i in range(mine)
    ]
    streams = [item[1] for item in turned_inputs]
    pieces = [[item[0]] for item in turned_inputs]
    for layer in range(2):
        vectors, qkv_shift, up_shift = smalls[layer]
        gain_one, bias_one, out_shift, gain_two, bias_two, down_shift = vectors
        first, second, up, down = weights[layer]
        begun = []
        for batch in everyone:
            qkv, attended, lse, parts = heads_forward(
                pieces[batch], first, second, qkv_shift, mask, heads, cols
            )
            begun.append((qkv, attended, lse, link.exchange(parts)))
            if layer == 0 and batch == 0:
                streams = after(streams, late)
                cotangents = [
                    turn_blocks([item[i] for item in late], None, None) for i in range(mine)
                ]
        middles = []
        for batch in everyone:
            middle, normed = add_and_norm(
                begun[batch][3], streams[batch], out_shift, gain_two, bias_two
            )
            middles.append((middle, link.spread(normed)))
        terms = []
        for batch in everyone:
            middle, twos = middles[batch]
            if layer == 0:
                hidden, slope, parts = feed_forward(twos, up, down, up_shift, cols)
                terms.append(link.exchange(parts))
            else:
                hidden, slope = feed_up(twos, up, up_shift)
            saved[layer][batch] = (
                streams[batch], pieces[batch], *begun[batch][:3], middle, twos, hidden, slope,
            )
        if layer == 0:
            streams, pieces = [], []
            for batch in everyone:
                stream, normed = add_and_norm(
                    terms[batch], middles[batch][0], down_shift, smalls[1][0][0], smalls[1][0][1]
                )
                streams.append(stream)
                pieces.append(link.spread(normed))

    def to_features(pair):
        blocks_out = jnp.stack([item.reshape(cols, width, own) for item in pair], axis=1)
        blocks_in = lax.all_to_all(blocks_out, "col", split_axis=0, concat_axis=0, tiled=True)
        return blocks_in.transpose(1, 2, 0, 3).reshape(len(pair), width, rows)

    def scatter_rows(grad):
        return lax.psum_scatter(grad, ("row", "section"), scatter_dimension=0, tiled=True)

    def all_heads_grad(qkv_grads):
        return weight_grad(
            [
                (saved[layer][0][1] + saved[layer][1][1], qkv_grads),
                (mids[0] + mids[1], [saved[layer][batch][3] for batch in everyone]),
            ]
        )

    reduced = [None, None]
    wide_sums = [None, None]
    narrow_sums = [None, None]
    ups = [[item[0]] for item in cotangents]
    bases = [item[1] for item in cotangents]
    base_sum = sum(jnp.sum(base, axis=0, keepdims=True) for base in bases)
    results = []
    turned = []
    for layer in (1, 0):
        vectors = smalls[layer][0]
        gain_one, gain_two = vectors[0], vectors[3]
        first, second, up, down = weights[layer]
        mids = []
        hidden_grads = []
        qkv_grads = []
        sums = []
        head_sums = []
        up_sums = []
        next_bases = []
        next_ups = []
        down_job = (ups[0] + ups[1], [saved[layer][batch][7] for batch in everyone])
        if layer == 1:
            down_grad = weight_grad([down_job])
            down_sum = scatter_rows(down_grad)
        terms = []
        for batch in everyone:
            slope = saved[layer][batch][8]
            slope = after(slope, down_grad if layer == 1 else (first_sum, heads_grad))
            hidden_grad, hidden_sum, parts = feed_backward(ups[batch], up, down, slope, cols)
            hidden_grads.append(hidden_grad)
            up_sums.append(hidden_sum[0])
            terms.append(link.exchange(parts))
        if layer == 0:
            down_grad = weight_grad([(after(down_job[0], hidden_grads), down_job[1])])
            down_sum = scatter_rows(down_grad)
        middle_grads = []
        seconds = []
        for batch in everyone:
            middle = saved[layer][batch][5]
            middle_grad, half, second_sums = norm_backward(
                terms[batch], middle, bases[batch], gain_two, False,
                layer * 15000000000 + (1 - layer) * 15000000000,
            )
            middle_grads.append(middle_grad)
            seconds.append(second_sums)
            mids.append(link.spread(half))
            if batch == 0:
                up_job = (saved[layer][0][6] + saved[layer][1][6], after(hidden_grads, half))
                up_grad = weight_grad([up_job])
                up_sum = scatter_rows(up_grad)
        terms = []
        for batch in everyone:
            qkv, lse = saved[layer][batch][2], saved[layer][batch][4]
            lse = after(lse, up_grad, reduced[1][2] if layer == 0 else ())
            qkv_grad, head_sum, parts = heads_backward(
                mids[batch], first, second, qkv, lse, mask, heads, cols,
                (1 - layer) * 15000000000,
            )
            qkv_grads.append(qkv_grad)
            head_sums.append(head_sum.reshape(-1))
            terms.append(link.exchange(parts))
        if layer == 0:
            heads_grad = all_heads_grad(qkv_grads)
        for batch in everyone:
            stream = saved[layer][batch][0]
            if layer == 0:
                stream = after(stream, heads_grad)
            stream_grad, half, first_sums = norm_backward(
                terms[batch], stream, middle_grads[batch], gain_one, layer == 0, layer * 15000000000
            )
            second_sums = seconds[batch]
            next_bases.append(stream_grad)
            if layer == 1:
                next_ups.append(link.spread(half))
                if batch == 0:
                    heads_grad = all_heads_grad(after(qkv_grads, half))
            else:
                turned.append(half)
            sums.append((first_sums, second_sums))
        wide_sum = jnp.concatenate([down_sum, up_sum], axis=1)
        first_sum = (down_sum, up_sum) if layer == 1 else None
        if layer == 0:
            heads_grad = after(heads_grad, down_sum, up_sum, turned)
        reduced[layer] = (wide_sum, up_sum, scatter_rows(heads_grad))
        first_sums = sums[0][0] + sums[1][0]
        second_sums = sums[0][1] + sums[1][1]
        wide_sums[layer] = jnp.concatenate(
            [first_sums[:2], second_sums[2:3], second_sums[:2], base_sum], axis=0
        )
        base_sum = first_sums[2:3]
        narrow_sums[layer] = jnp.concatenate(
            [head_sums[0] + head_sums[1], up_sums[0] + up_sums[1]]
        )
        bases = next_bases
        ups = next_ups


    last_parts = feed_last(
        after([saved[1][batch][7] for batch in everyone], turned),
        [saved[1][batch][5] for batch in everyone],
        smalls[1][0][5],
        weights[1][3],
    )
    outputs = []
    for batch in everyone:
        terms = link.exchange(last_parts[batch])
        outputs.append(sum([term.astype(F32) for term in terms[1:]], terms[0].astype(F32)))
    outputs = jnp.stack(outputs).astype(BF)

    wide_sums = after(wide_sums, last_parts)
    wide_both = jnp.stack(wide_sums).reshape(2, 6, cols, width)
    wide_here = lax.dynamic_index_in_dim(wide_both, col, 2, keepdims=False)
    for j in range(1, cols):
        wide_here = wide_here + xor_step(
            lax.dynamic_index_in_dim(wide_both, col ^ j, 2, keepdims=False), "col", j
        )
    small_sums = jnp.concatenate([wide_here.reshape(2, -1), jnp.stack(narrow_sums)], axis=1)
    small_own = lax.dynamic_index_in_dim(small_sums, section, 0, keepdims=False)
    small_own = small_own + swap_section(
        lax.dynamic_index_in_dim(small_sums, 1 - section, 0, keepdims=False)
    )
    step = 1
    while step < lax.axis_size("row"):
        small_own = small_own + xor_step(small_own, "row", step)
        step *= 2
    small_out = small_own[: 6 * width].reshape(6, width)
    head_out = small_own[6 * width : 6 * width + 2 * wide].reshape(2, wide)
    head_out = split_heads(
        head_out, previous_column(tail_columns(head_out, width, col)), width, col
    )
    up_bias_grad = small_own[6 * width + 2 * wide :]

    def settle(first_half, second_half):
        got = swap_section(jnp.where(is_first, second_half, first_half))
        keep = jnp.where(is_first, first_half, second_half)
        low = jnp.where(is_first, keep, got)
        high = jnp.where(is_first, got, keep)
        return jnp.concatenate([low, high], axis=0)

    wide_out = settle(reduced[0][0], reduced[1][0])
    down_out = wide_out[:, : wide_out.shape[1] // 2].astype(F32)
    up_out = wide_out[:, wide_out.shape[1] // 2 :].astype(F32)

    def by_matrix(flat):
        return jnp.stack([flat[:, i * wide : (i + 1) * wide] for i in range(4)])

    keep = by_matrix(jnp.where(is_first, reduced[0][2], reduced[1][2]))
    send = by_matrix(jnp.where(is_first, reduced[1][2], reduced[0][2]))
    got = swap_section(send)
    keep_before = previous_column(tail_columns(keep, width, col))
    got_before = previous_column_across(tail_columns(send, width, col))
    keep = split_heads(keep, keep_before, width, col)
    got = split_heads(got, got_before, width, col)
    heads_out = jnp.concatenate(
        [jnp.where(is_first, keep, got), jnp.where(is_first, got, keep)], axis=1
    ).astype(F32)

    grads = to_features(turned)
    got = swap_section(jnp.where(is_first, outputs, grads))
    keep = jnp.where(is_first, grads, outputs)
    boundary = jnp.concatenate(
        [jnp.where(is_first, keep, got), jnp.where(is_first, got, keep)], axis=0
    ).astype(F32)

    return (
        boundary[None],
        small_out[0][None],
        small_out[1][None],
        heads_out[0][None],
        heads_out[1][None],
        heads_out[2][None],
        head_out[0][None],
        head_out[1][None],
        heads_out[3].T[None],
        small_out[2][None],
        small_out[3][None],
        small_out[4][None],
        up_out[None],
        up_bias_grad[None],
        down_out[None],
        small_out[5][None],
    )


def solution(mesh):
    vector = P("section", "col")
    matrix = P("section", "row", "col")
    turned = P("section", "col", "row")
    plane = P(None, "col", "row")
    in_specs = (
        plane, plane, P(), vector, vector, matrix, matrix, matrix, vector, vector,
        turned, vector, vector, vector, matrix, vector, matrix, vector,
    )
    out_specs = (
        P("section", None, "col", "row"), vector, vector, matrix, matrix, matrix, vector, vector,
        turned, vector, vector, vector, matrix, vector, matrix, vector,
    )
    return jax.shard_map(
        on_device, mesh=mesh, in_specs=in_specs, out_specs=out_specs, check_vma=False
    )
```

```python
import functools
import math

import jax
import jax.numpy as jnp
from jax import lax
from jax.experimental import pallas as pl
from jax.experimental.pallas import tpu as pltpu
from jax.sharding import PartitionSpec as P

H = 25
HD = 64
L = 512
BF = jnp.bfloat16
F32 = jnp.float32

epsilon = 1e-05
tanh_scale = math.sqrt(2.0 / math.pi)
cubic_weight = 0.044715
score_scale = HD ** (-0.5)


def xor_step(value, axis, step):
    count = lax.axis_size(axis)
    return lax.ppermute(value, axis, [(i, i ^ step) for i in range(count)])


class Link:
    def move(self, parts):
        return [xor_step(part, "col", j + 1) for j, part in enumerate(parts)]

    def spread(self, rows, axis=0):
        count = lax.axis_size("col")
        if count != 4:
            return [rows] + self.move([rows] * (count - 1))
        half = rows.shape[axis] // 2
        one, two = xor_step(rows, "col", 1), xor_step(rows, "col", 2)
        low = xor_step(lax.slice_in_dim(two, 0, half, axis=axis), "col", 1)
        high = xor_step(lax.slice_in_dim(one, half, 2 * half, axis=axis), "col", 2)
        return [rows, one, two, low, high]

    def exchange(self, parts):
        return [parts[0]] + self.move(list(parts[1:]))


def after(values, *tokens):
    return lax.optimization_barrier((values, tokens))[0]


def swap_section(value):
    return xor_step(value, "section", 1)


def xor_order(stack, index):
    count = stack.shape[0]
    return jnp.stack(
        [lax.dynamic_index_in_dim(stack, index ^ t, 0, keepdims=False) for t in range(count)]
    )


def head_share():
    count = lax.axis_size("col")
    return H // count, (H // count + 1) * HD


def head_shift(col_index):
    count = lax.axis_size("col")
    return jnp.where(col_index == 0, 0, HD - (HD // count) * col_index)


def next_column(value):
    count = lax.axis_size("col")
    return lax.ppermute(value, "col", [(i + 1, i) for i in range(count - 1)])


def next_column_across(value):
    count = lax.axis_size("col")
    pairs = [
        ((1 - s) * count + i + 1, s * count + i) for s in range(2) for i in range(count - 1)
    ]
    return lax.ppermute(value, ("section", "col"), pairs)


def join_heads(columns, following, col_index):
    per, wide = head_share()
    lead = columns.shape[:-1]
    pad = max(0, wide - columns.shape[-1])
    extended = jnp.concatenate(
        [columns, following, jnp.zeros(lead + (pad,), columns.dtype)], axis=-1
    )
    moved = lax.dynamic_slice_in_dim(
        extended, head_shift(col_index), wide, axis=extended.ndim - 1
    )
    limit = jnp.where(col_index == 0, wide, per * HD)
    return jnp.where(jnp.arange(wide) < limit, moved, jnp.zeros((), moved.dtype))


def align_heads(columns, col_index):
    return join_heads(columns, next_column(columns[..., :HD]), col_index)


def tail_columns(columns, width, col_index):
    begin = width - head_shift(col_index)
    padded = jnp.concatenate(
        [columns, jnp.zeros(columns.shape[:-1] + (HD,), columns.dtype)], axis=-1
    )
    return lax.dynamic_slice_in_dim(padded, begin, HD, axis=columns.ndim - 1)


def split_heads(columns, before, width, col_index):
    shift = head_shift(col_index)
    pad = jnp.zeros(columns.shape[:-1] + (HD,), columns.dtype)
    joined = jnp.concatenate([before, columns, pad], axis=-1)
    rest = lax.dynamic_slice_in_dim(joined, HD - shift, width, axis=columns.ndim - 1)
    fill = jnp.zeros(columns.shape[:-1] + (width - HD,), columns.dtype)
    front = jnp.concatenate([before, fill], axis=-1)
    return jnp.where(jnp.arange(width) < shift, front, rest)


def previous_column(value):
    count = lax.axis_size("col")
    return lax.ppermute(value, "col", [(i, i + 1) for i in range(count - 1)])


def previous_column_across(value):
    count = lax.axis_size("col")
    pairs = [
        ((1 - s) * count + i, s * count + i + 1) for s in range(2) for i in range(count - 1)
    ]
    return lax.ppermute(value, ("section", "col"), pairs)


def contract(left, right, left_dim, right_dim):
    return lax.dot_general(
        left, right, (((left_dim,), (right_dim,)), ((), ())), preferred_element_type=F32
    )


def call(kernel, outs, args, scratch=(), flops=0, exps=0, anywhere=()):
    nbytes = sum(math.prod(x.shape) * x.dtype.itemsize for x in list(args) + list(outs))
    return pl.pallas_call(
        kernel,
        out_shape=tuple(outs),
        in_specs=[
            pl.BlockSpec(memory_space=pl.ANY if i in anywhere else pltpu.VMEM)
            for i in range(len(args))
        ],
        out_specs=tuple(pl.BlockSpec(memory_space=pltpu.VMEM) for _ in outs),
        scratch_shapes=list(scratch),
        compiler_params=pltpu.CompilerParams(vmem_limit_bytes=44 * 1024 * 1024),
        cost_estimate=pl.CostEstimate(flops=int(flops * WEIGHT), bytes_accessed=0, transcendentals=0),
    )(*args)


def shape(dims, kind):
    return jax.ShapeDtypeStruct(dims, kind)


class Matrix:
    def __init__(self, array, runs):
        self.array, self.runs = array, runs

    @property
    def dims(self):
        return (sum(run[2] for run in self.runs), self.array.shape[1])

    def copies(self, source, target, sems):
        return [
            pltpu.make_async_copy(
                source.at[pl.ds(begin, size), :], target.at[pl.ds(to, size), :], sems.at[i]
            )
            for i, (begin, to, size) in enumerate(self.runs)
        ]

    def scratch(self):
        return [pltpu.VMEM(self.dims, BF), pltpu.SemaphoreType.DMA((len(self.runs),))]


def fetch(matrices, sources, held):
    waits = []
    for matrix, source, (target, sems) in zip(matrices, sources, held):
        copies = matrix.copies(source, target, sems)
        for copy in copies:
            copy.start()
        waits.append(copies)
    return waits


def finish(copies):
    for copy in copies:
        copy.wait()


def stack_pieces(pieces, whole):
    begin = 0
    for piece in pieces:
        whole[begin : begin + piece.shape[0], :] = piece[...]
        begin += piece.shape[0]


def store_parts(parts, begin, value):
    here = parts[0].shape[0]
    for i in range(value.shape[0] // here):
        parts[begin // here + i][...] = value[i * here : (i + 1) * here].astype(BF)


CHUNK = 256
WEIGHT = 4


def heads_forward(pieces, first, second, bias, mask, heads, parts):
    rows = mask.shape[0]
    features = pieces[0].shape[1]
    wide = heads * HD
    count = len(pieces)

    def kernel(*refs):
        piece_refs, refs = refs[:count], refs[count:]
        first_hbm, second_hbm, bias_ref, mask_ref, qkv_ref, out_ref, lse_ref = refs[:7]
        part_refs, refs = refs[7 : 7 + parts], refs[7 + parts :]
        whole, first_ref, first_sem, second_ref, second_sem = refs
        waits = fetch(
            (first, second),
            (first_hbm, second_hbm),
            ((first_ref, first_sem), (second_ref, second_sem)),
        )
        stack_pieces(piece_refs, whole)
        finish(waits[0])
        for begin in range(0, rows, CHUNK):
            some = slice(begin, begin + CHUNK)
            value = contract(whole[some, :], first_ref[...], 1, 0) + bias_ref[:, : 2 * wide]
            qkv_ref[some, : 2 * wide] = value.astype(BF)
        finish(waits[1])
        for begin in range(0, rows, CHUNK):
            some = slice(begin, begin + CHUNK)
            value = contract(whole[some, :], second_ref[:, :wide], 1, 0) + bias_ref[:, 2 * wide :]
            qkv_ref[some, 2 * wide :] = value.astype(BF)
        for head in range(heads):
            low = head * HD
            key = qkv_ref[:, wide + low : wide + low + HD]
            value = qkv_ref[:, 2 * wide + low : 2 * wide + low + HD]
            for begin in range(0, rows, CHUNK):
                part = pl.ds(begin, CHUNK)
                query = qkv_ref[part, low : low + HD] * jnp.asarray(score_scale, BF)
                scores = contract(key, query, 1, 1) + mask_ref[:, part]
                peak = jnp.max(scores, axis=0, keepdims=True)
                weights = jnp.exp(scores - peak)
                mass = jnp.sum(weights, axis=0, keepdims=True)
                lse_ref[head : head + 1, part] = peak + jnp.log(mass)
                mixed = contract(value, weights.astype(BF), 0, 0) / mass
                out_ref[part, low : low + HD] = mixed.T.astype(BF)
        for begin in range(0, rows, CHUNK):
            some = slice(begin, begin + CHUNK)
            store_parts(part_refs, begin, contract(out_ref[some, :], second_ref[:, wide:], 1, 1))

    here = rows // parts
    result = call(
        kernel,
        [shape((rows, 3 * wide), BF), shape((rows, wide), BF), shape((heads, rows), F32)]
        + [shape((here, features), BF)] * parts,
        list(pieces) + [first.array, second.array, bias, mask],
        [pltpu.VMEM((rows, features), BF)] + first.scratch() + second.scratch(),
        flops=8 * rows * features * wide + 16 * rows * rows * wide,
        exps=rows * rows * heads,
        anywhere=(count, count + 1),
    )
    return result[0], result[1], result[2], result[3:]


def heads_backward(pieces, first, second, qkv, lse, mask, heads, parts, weight):
    rows = mask.shape[0]
    features = pieces[0].shape[1]
    wide = heads * HD
    count = len(pieces)

    def kernel(*refs):
        piece_refs, refs = refs[:count], refs[count:]
        first_hbm, second_hbm, qkv_ref, lse_ref, mask_ref, grad_ref, sum_ref = refs[:7]
        part_refs, refs = refs[7 : 7 + parts], refs[7 + parts :]
        whole, up_ref, first_ref, first_sem, second_ref, second_sem = refs
        waits = fetch(
            (second, first),
            (second_hbm, first_hbm),
            ((second_ref, second_sem), (first_ref, first_sem)),
        )
        stack_pieces(piece_refs, whole)
        finish(waits[0])
        for begin in range(0, rows, CHUNK):
            some = slice(begin, begin + CHUNK)
            up_ref[some, :] = contract(whole[some, :], second_ref[:, wide:], 1, 0).astype(BF)
        for head in range(heads):
            low = head * HD
            key = qkv_ref[:, wide + low : wide + low + HD]
            value = qkv_ref[:, 2 * wide + low : 2 * wide + low + HD]
            key_grad = jnp.zeros((rows, HD), F32)
            value_grad = jnp.zeros((rows, HD), F32)
            query_sum = jnp.zeros((1, HD), F32)
            for begin in range(0, rows, CHUNK):
                part = pl.ds(begin, CHUNK)
                query = qkv_ref[part, low : low + HD] * jnp.asarray(score_scale, BF)
                up = up_ref[part, low : low + HD]
                scores = contract(key, query, 1, 1) + mask_ref[:, part]
                weights = jnp.exp(scores - lse_ref[head : head + 1, part])
                value_grad = value_grad + contract(weights.astype(BF), up, 1, 0)
                slope = contract(value, up, 1, 1)
                delta = jnp.sum(weights * slope, axis=0, keepdims=True)
                scores_grad = (weights * (slope - delta)).astype(BF)
                key_grad = key_grad + contract(scores_grad, query, 1, 0)
                query_grad = (contract(key, scores_grad, 0, 0) * score_scale).T.astype(BF)
                grad_ref[part, low : low + HD] = query_grad
                query_sum = query_sum + jnp.sum(query_grad.astype(F32), axis=0, keepdims=True)
            grad_ref[:, wide + low : wide + low + HD] = key_grad.astype(BF)
            grad_ref[:, 2 * wide + low : 2 * wide + low + HD] = value_grad.astype(BF)
            sum_ref[0:1, low : low + HD] = query_sum
            sum_ref[1:2, low : low + HD] = jnp.sum(value_grad, axis=0, keepdims=True)
        finish(waits[1])
        for begin in range(0, rows, CHUNK):
            some = slice(begin, begin + CHUNK)
            value = contract(grad_ref[some, : 2 * wide], first_ref[...], 1, 1)
            value = value + contract(grad_ref[some, 2 * wide :], second_ref[:, :wide], 1, 1)
            store_parts(part_refs, begin, value)

    here = rows // parts
    result = call(
        kernel,
        [shape((rows, 3 * wide), BF), shape((2, wide), F32)]
        + [shape((here, features), BF)] * parts,
        list(pieces) + [first.array, second.array, qkv, lse, mask],
        [pltpu.VMEM((rows, features), BF), pltpu.VMEM((rows, wide), BF)]
        + first.scratch()
        + second.scratch(),
        flops=8 * rows * features * wide + 40 * rows * rows * wide + weight,
        exps=rows * rows * heads,
        anywhere=(count, count + 1),
    )
    return result[0], result[1], result[2:]


def gelu_both(inputs):
    inner = tanh_scale * (inputs + cubic_weight * inputs * inputs * inputs)
    tangent = jnp.tanh(inner)
    value = 0.5 * inputs * (1.0 + tangent)
    slope = 0.5 * (1.0 + tangent) + 0.5 * inputs * (1.0 - tangent * tangent) * tanh_scale * (
        1.0 + 3.0 * cubic_weight * inputs * inputs
    )
    return value.astype(BF), slope.astype(BF)


def feed_up(pieces, up, bias):
    rows = sum(piece.shape[0] for piece in pieces)
    features = pieces[0].shape[1]
    hidden = up.dims[1]
    count = len(pieces)

    def kernel(*refs):
        piece_refs, refs = refs[:count], refs[count:]
        up_hbm, bias_ref, hidden_ref, slope_ref, whole, up_ref, up_sem = refs
        (wait,) = fetch((up,), (up_hbm,), ((up_ref, up_sem),))
        stack_pieces(piece_refs, whole)
        finish(wait)
        for begin in range(0, rows, CHUNK):
            some = slice(begin, begin + CHUNK)
            value, slope = gelu_both(contract(whole[some, :], up_ref[...], 1, 0) + bias_ref[...])
            hidden_ref[some, :] = value
            slope_ref[some, :] = slope

    return call(
        kernel,
        [shape((rows, hidden), BF)] * 2,
        list(pieces) + [up.array, bias],
        [pltpu.VMEM((rows, features), BF)] + up.scratch(),
        flops=2 * rows * features * hidden,
        anywhere=(count,),
    )


def feed_last(hiddens, middles, shift, down):
    rows, units = hiddens[0].shape
    own, features = middles[0].shape
    cols = rows // own
    width = features // cols
    count = len(hiddens)

    def kernel(*refs):
        hidden_refs, refs = refs[:count], refs[count:]
        middle_refs, refs = refs[:count], refs[count:]
        shift_ref, down_hbm = refs[:2]
        part_refs, refs = refs[2 : 2 + count * cols], refs[2 + count * cols :]
        ordered, whole, down_ref, down_sem = refs
        (wait,) = fetch((down,), (down_hbm,), ((down_ref, down_sem),))
        here = lax.axis_index("col")
        finish(wait)
        for i in range(count):
            for t in range(cols):
                start = pl.multiple_of((here ^ t) * own, own)
                ordered[t * own : (t + 1) * own, :] = hidden_refs[i][pl.ds(start, own), :]
            base = (middle_refs[i][...] + shift_ref[...]).T
            for begin in range(0, features, width):
                some = slice(begin, begin + width)
                value = contract(down_ref[some, :], ordered[...], 1, 1)
                for t in range(cols):
                    tokens = slice(t * own, (t + 1) * own)
                    extra = jnp.where(here == t, base[some, :], 0.0)
                    whole[some, tokens] = value[:, tokens] + extra
            for j in range(cols):
                start = pl.multiple_of((here ^ j) * width, 8)
                part_refs[i * cols + j][...] = whole[pl.ds(start, width), :].astype(BF)

    result = call(
        kernel,
        [shape((width, rows), BF)] * (count * cols),
        list(hiddens) + list(middles) + [shift, down.array],
        [pltpu.VMEM((rows, units), BF), pltpu.VMEM((features, rows), F32)] + down.scratch(),
        flops=2 * count * rows * features * units,
        anywhere=(2 * count + 1,),
    )
    return [result[i * cols : (i + 1) * cols] for i in range(count)]


def feed_forward(pieces, up, down, bias, parts):
    rows = sum(piece.shape[0] for piece in pieces)
    features = pieces[0].shape[1]
    hidden = up.dims[1]
    count = len(pieces)

    def kernel(*refs):
        piece_refs, refs = refs[:count], refs[count:]
        up_hbm, down_hbm, bias_ref, hidden_ref, slope_ref = refs[:5]
        part_refs, refs = refs[5 : 5 + parts], refs[5 + parts :]
        whole, up_ref, up_sem, down_ref, down_sem = refs
        waits = fetch(
            (up, down), (up_hbm, down_hbm), ((up_ref, up_sem), (down_ref, down_sem))
        )
        stack_pieces(piece_refs, whole)
        finish(waits[0])
        for begin in range(0, rows, CHUNK):
            some = slice(begin, begin + CHUNK)
            value, slope = gelu_both(contract(whole[some, :], up_ref[...], 1, 0) + bias_ref[...])
            hidden_ref[some, :] = value
            slope_ref[some, :] = slope
        finish(waits[1])
        for begin in range(0, rows, CHUNK):
            some = slice(begin, begin + CHUNK)
            store_parts(part_refs, begin, contract(hidden_ref[some, :], down_ref[...], 1, 1))

    here = rows // parts
    result = call(
        kernel,
        [shape((rows, hidden), BF)] * 2 + [shape((here, features), BF)] * parts,
        list(pieces) + [up.array, down.array, bias],
        [pltpu.VMEM((rows, features), BF)] + up.scratch() + down.scratch(),
        flops=4 * rows * features * hidden,
        exps=rows * hidden,
        anywhere=(count, count + 1),
    )
    return result[0], result[1], result[2:]


def feed_backward(pieces, up, down, slope, parts):
    rows = sum(piece.shape[0] for piece in pieces)
    features = pieces[0].shape[1]
    hidden = up.dims[1]
    count = len(pieces)

    def kernel(*refs):
        piece_refs, refs = refs[:count], refs[count:]
        up_hbm, down_hbm, slope_ref, grad_ref, sum_ref = refs[:5]
        part_refs, refs = refs[5 : 5 + parts], refs[5 + parts :]
        whole, up_ref, up_sem, down_ref, down_sem = refs
        waits = fetch(
            (down, up), (down_hbm, up_hbm), ((down_ref, down_sem), (up_ref, up_sem))
        )
        stack_pieces(piece_refs, whole)
        finish(waits[0])
        for begin in range(0, rows, CHUNK):
            some = slice(begin, begin + CHUNK)
            value = contract(whole[some, :], down_ref[...], 1, 0) * slope_ref[some, :].astype(F32)
            grad_ref[some, :] = value.astype(BF)
            add = jnp.sum(value, axis=0, keepdims=True)
            sum_ref[...] = add if begin == 0 else sum_ref[...] + add
        finish(waits[1])
        for begin in range(0, rows, CHUNK):
            some = slice(begin, begin + CHUNK)
            store_parts(part_refs, begin, contract(grad_ref[some, :], up_ref[...], 1, 1))

    here = rows // parts
    result = call(
        kernel,
        [shape((rows, hidden), BF), shape((1, hidden), F32)]
        + [shape((here, features), BF)] * parts,
        list(pieces) + [up.array, down.array, slope],
        [pltpu.VMEM((rows, features), BF)] + up.scratch() + down.scratch(),
        flops=4 * rows * features * hidden,
        anywhere=(count, count + 1),
    )
    return result[0], result[1], result[2:]


def weight_grad(jobs):
    args = []
    for lefts, rights in jobs:
        args += list(lefts) + list(rights)
    features = jobs[0][0][0].shape[1]
    rows = sum(right.shape[0] for right in jobs[0][1])
    widths = [rights[0].shape[1] for _, rights in jobs]
    chunk = features // 4

    def kernel(*refs):
        refs = list(refs)
        turned, joined = refs[-2], refs[-1]
        out_ref = refs[len(args)]
        at = 0
        column = 0
        for (lefts, rights), width in zip(jobs, widths):
            begin = 0
            for _ in lefts:
                left = refs[at]
                at += 1
                turned[:, begin : begin + left.shape[0]] = left[...].T
                begin += left.shape[0]
            begin = 0
            for _ in rights:
                right = refs[at]
                at += 1
                joined[begin : begin + right.shape[0], :width] = right[...]
                begin += right.shape[0]

            for i in range(4):
                some = slice(i * chunk, (i + 1) * chunk)
                value = contract(turned[some, :], joined[:, :width], 1, 0)
                out_ref[some, column : column + width] = value.astype(BF)
            column += width

    return call(
        kernel,
        [shape((features, sum(widths)), BF)],
        args,
        [pltpu.VMEM((features, rows), BF), pltpu.VMEM((rows, max(widths)), BF)],
        flops=2 * rows * features * sum(widths),
    )[0]


def row_stats(stream):
    mean = jnp.mean(stream, axis=1, keepdims=True)
    scale = lax.rsqrt(jnp.mean(stream * stream, axis=1, keepdims=True) - mean * mean + epsilon)
    return mean, scale


def norm(stream, gain, offset):
    mean, scale = row_stats(stream)
    return (((stream - mean) * scale) * gain + offset).astype(BF)


def sum_refs(refs):
    value = refs[0][...].astype(F32)
    for ref in refs[1:]:
        value = value + ref[...].astype(F32)
    return value


def turn_blocks(blocks, gain, offset):
    count = len(blocks)
    width, rows = blocks[0].shape
    cols = lax.axis_size("col")
    own = rows // cols
    normed = gain is not None
    vectors = [gain, offset] if normed else []

    def kernel(*refs):
        block_refs, refs = refs[:count], refs[count:]
        vector_refs, refs = refs[: len(vectors)], refs[len(vectors) :]
        out_ref, own_ref, held = refs[0], refs[1], refs[-1]
        whole = refs[2] if normed else out_ref
        here = lax.axis_index("col")
        at = 0
        for block_ref in block_refs:
            columns = block_ref.shape[1]
            held[at // rows, :, at % rows : at % rows + columns] = block_ref[...]
            at += columns
        for t in range(cols):
            plane = held[here ^ t].T
            for i in range(cols):
                start = pl.multiple_of((here ^ i) * own, own)
                whole[pl.ds(start, own), t * width : (t + 1) * width] = plane[
                    i * own : (i + 1) * own
                ]
        own_ref[...] = whole[:own, :].astype(F32)
        if normed:
            for begin in range(0, rows, own):
                some = slice(begin, begin + own)
                value = whole[some, :].astype(F32)
                out_ref[some, :] = norm(value, vector_refs[0][...], vector_refs[1][...])

    full = (rows, width * cols)
    scratch = [pltpu.VMEM(full, BF)] if normed else []
    return call(
        kernel,
        [shape(full, BF), shape((own, full[1]), F32)],
        list(blocks) + vectors,
        scratch + [pltpu.VMEM((cols, width, rows), BF)],
    )


def add_and_norm(terms, stream, shift, gain, offset):
    count = len(terms)

    def kernel(*refs):
        stream_ref, shift_ref, gain_ref, offset_ref, sum_ref, norm_ref = refs[count:]
        value = stream_ref[...] + sum_refs(refs[:count]) + shift_ref[...]
        sum_ref[...] = value
        norm_ref[...] = norm(value, gain_ref[...], offset_ref[...])

    return call(
        kernel,
        [shape(stream.shape, F32), shape(stream.shape, BF)],
        list(terms) + [stream, shift, gain, offset],
    )


def norm_backward(terms, stream, base, gain, turn, weight):
    count = len(terms)

    def kernel(*refs):
        stream_ref, base_ref, gain_ref, out_ref, half_ref, sum_ref = refs[count:]
        incoming = sum_refs(refs[:count])
        value = stream_ref[...]
        mean, scale = row_stats(value)
        normed = (value - mean) * scale
        scaled = incoming * gain_ref[...]
        outgoing = base_ref[...] + scale * (
            scaled
            - jnp.mean(scaled, axis=1, keepdims=True)
            - normed * jnp.mean(scaled * normed, axis=1, keepdims=True)
        )
        out_ref[...] = outgoing
        half_ref[...] = outgoing.T.astype(BF) if turn else outgoing.astype(BF)
        sum_ref[0:1, :] = jnp.sum(incoming * normed, axis=0, keepdims=True)
        sum_ref[1:2, :] = jnp.sum(incoming, axis=0, keepdims=True)
        sum_ref[2:3, :] = jnp.sum(outgoing, axis=0, keepdims=True)

    dims = stream.shape
    return call(
        kernel,
        [shape(dims, F32), shape(dims[::-1] if turn else dims, BF), shape((3, dims[1]), F32)],
        list(terms) + [stream, base, gain],
        flops=weight,
    )


def on_device(
    block_input,
    out_cotangent,
    group_order,
    first_gain,
    first_bias,
    query_weight,
    key_weight,
    value_weight,
    query_bias,
    value_bias,
    out_weight,
    out_bias,
    second_gain,
    second_bias,
    up_weight,
    up_bias,
    down_weight,
    down_bias,
):
    section = lax.axis_index("section")
    col = lax.axis_index("col")
    cols = lax.axis_size("col")
    batches, width, rows = block_input.shape
    own = rows // cols
    mine = batches // 2
    per, wide = head_share()
    heads = wide // HD
    features = width * cols
    is_first = section == 0

    def gather_block(own_part):
        full = lax.all_gather(own_part, ("row", "section"), axis=0, tiled=True)
        return full, own_part.shape[0], full.shape[0] // (2 * own_part.shape[0])

    def gather_pair(own_part):
        full, block, count = gather_block(own_part)
        if block % 16 == 0:
            return tuple(
                Matrix(full, [((2 * i + k) * block, i * block, block) for i in range(count)])
                for k in range(2)
            )
        full = full.reshape(count, 2, block, -1)
        both = [full[:, k].reshape(count * block, -1) for k in range(2)]
        return tuple(Matrix(one, [(0, 0, count * block)]) for one in both)

    def gather_halves(own_part, block):
        full, low, count = gather_block(own_part)
        high = block - low
        if low % 16 == 0 and high % 16 == 0:
            runs = []
            for i in range(count):
                runs.append((2 * i * low, i * block, low))
                runs.append(((2 * i + 1) * low, i * block + low, high))
            return Matrix(full, runs)
        full = full.reshape(count, 2 * low, -1)[:, :block].reshape(count * block, -1)
        return Matrix(full, [(0, 0, count * block)])

    pair_one = jnp.stack([query_weight[0], key_weight[0]])
    pair_two = jnp.stack([value_weight[0], out_weight[0].T])
    keep = jnp.where(is_first, pair_one, pair_two)
    send = jnp.where(is_first, pair_two, pair_one)
    got = swap_section(send)
    keep_after = next_column(keep[..., :HD])
    got_after = next_column_across(send[..., :HD])
    keep = join_heads(keep, keep_after, col)
    got = join_heads(got, got_after, col)
    heads_parts = [
        jnp.concatenate([item[0], item[1]], axis=1)
        for item in (jnp.where(is_first, keep, got), jnp.where(is_first, got, keep))
    ]
    block = up_weight.shape[1]
    low = block // 2
    low += -low % 16 if block % 16 == 0 else 0

    def exchange_wide(up_own, down_own):
        fill = jnp.zeros((2 * low - block, up_own.shape[1]), BF)
        lows = jnp.concatenate([up_own[:low], down_own[:low]])
        got = swap_section(jnp.where(is_first, jnp.concatenate([down_own, fill]), lows))
        first_layer = jnp.where(is_first, up_own, got[:block])
        seconds = [
            jnp.where(is_first, got[begin : begin + low], jnp.concatenate([item[low:], fill]))
            for begin, item in ((0, up_own), (low, down_own))
        ]
        return first_layer, seconds

    small_wide = jnp.stack(
        [first_gain[0], first_bias[0], out_bias[0], second_gain[0], second_bias[0], down_bias[0]]
    )
    small_wide = xor_order(
        jnp.stack([small_wide] + [xor_step(small_wide, "col", j) for j in range(1, cols)]), col
    )
    small_wide = jnp.swapaxes(small_wide, 0, 1).reshape(6, features)
    small_heads = align_heads(jnp.stack([query_bias[0], value_bias[0]]), col).reshape(-1)
    small_own = jnp.concatenate([small_wide.reshape(-1), small_heads, up_bias[0]])
    small_other = swap_section(small_own)
    small_layers = (
        jnp.where(is_first, small_own, small_other),
        jnp.where(is_first, small_other, small_own),
    )

    def smalls_of(layer):
        flat = small_layers[layer]
        vectors = flat[: 6 * features].reshape(6, features)
        query_shift = flat[6 * features : 6 * features + wide]
        value_shift = flat[6 * features + wide : 6 * features + 2 * wide]
        qkv_shift = jnp.concatenate([query_shift, jnp.zeros((wide,), F32), value_shift])
        vectors = [vectors[i : i + 1] for i in range(6)]
        return vectors, qkv_shift[None], flat[6 * features + 2 * wide :][None]

    smalls = [smalls_of(0), smalls_of(1)]

    link = Link()
    input_own = lax.dynamic_slice_in_dim(block_input, section * mine, mine, 0)
    cotangent_own = lax.dynamic_slice_in_dim(out_cotangent, section * mine, mine, 0)
    early = link.spread(input_own, 2)
    late = link.spread(after(cotangent_own, early), 2)
    wide_first, wide_second = exchange_wide(
        *after((up_weight[0], down_weight[0]), heads_parts, early, small_layers)
    )

    blocks = group_order.shape[0]
    group_rows = L // blocks
    places = jnp.arange(rows, dtype=jnp.int32)
    places = ((places // own) ^ col) * own + places % own
    within = places % L
    match = (within // group_rows)[:, None] == jnp.arange(blocks, dtype=jnp.int32)[None, :]
    position = (
        jnp.sum(jnp.where(match, group_order[None, :], 0), axis=1) * group_rows
        + within % group_rows
    )
    sequence = places // L
    allowed = (sequence[:, None] == sequence[None, :]) & (position[:, None] <= position[None, :])
    mask = jnp.where(allowed, 0.0, -jnp.inf).astype(F32)

    everyone = range(mine)
    weights = [gather_pair(heads_parts[0]) + gather_pair(wide_first)]
    weights.append(
        gather_pair(heads_parts[1])
        + tuple(gather_halves(item, block) for item in wide_second)
    )
    saved = [[None] * mine, [None] * mine]
    turned_inputs = [
        turn_blocks([item[i] for item in early], smalls[0][0][0], smalls[0][0][1])
        for i in range(mine)
    ]
    streams = [item[1] for item in turned_inputs]
    pieces = [[item[0]] for item in turned_inputs]
    for layer in range(2):
        vectors, qkv_shift, up_shift = smalls[layer]
        gain_one, bias_one, out_shift, gain_two, bias_two, down_shift = vectors
        first, second, up, down = weights[layer]
        begun = []
        for batch in everyone:
            qkv, attended, lse, parts = heads_forward(
                pieces[batch], first, second, qkv_shift, mask, heads, cols
            )
            begun.append((qkv, attended, lse, link.exchange(parts)))
            if layer == 0 and batch == 0:
                streams = after(streams, late)
                cotangents = [
                    turn_blocks([item[i] for item in late], None, None) for i in range(mine)
                ]
        middles = []
        for batch in everyone:
            middle, normed = add_and_norm(
                begun[batch][3], streams[batch], out_shift, gain_two, bias_two
            )
            middles.append((middle, link.spread(normed)))
        terms = []
        for batch in everyone:
            middle, twos = middles[batch]
            if layer == 0:
                hidden, slope, parts = feed_forward(twos, up, down, up_shift, cols)
                terms.append(link.exchange(parts))
            else:
                hidden, slope = feed_up(twos, up, up_shift)
            saved[layer][batch] = (
                streams[batch], pieces[batch], *begun[batch][:3], middle, twos, hidden, slope,
            )
        if layer == 0:
            streams, pieces = [], []
            for batch in everyone:
                stream, normed = add_and_norm(
                    terms[batch], middles[batch][0], down_shift, smalls[1][0][0], smalls[1][0][1]
                )
                streams.append(stream)
                pieces.append(link.spread(normed))

    def to_features(pair):
        blocks_out = jnp.stack([item.reshape(cols, width, own) for item in pair], axis=1)
        blocks_in = lax.all_to_all(blocks_out, "col", split_axis=0, concat_axis=0, tiled=True)
        return blocks_in.transpose(1, 2, 0, 3).reshape(len(pair), width, rows)

    def scatter_rows(grad):
        return lax.psum_scatter(grad, ("row", "section"), scatter_dimension=0, tiled=True)

    def all_heads_grad(qkv_grads):
        return weight_grad(
            [
                (saved[layer][0][1] + saved[layer][1][1], qkv_grads),
                (mids[0] + mids[1], [saved[layer][batch][3] for batch in everyone]),
            ]
        )

    reduced = [None, None]
    wide_sums = [None, None]
    narrow_sums = [None, None]
    ups = [[item[0]] for item in cotangents]
    bases = [item[1] for item in cotangents]
    base_sum = sum(jnp.sum(base, axis=0, keepdims=True) for base in bases)
    results = []
    turned = []
    for layer in (1, 0):
        vectors = smalls[layer][0]
        gain_one, gain_two = vectors[0], vectors[3]
        first, second, up, down = weights[layer]
        mids = []
        hidden_grads = []
        qkv_grads = []
        sums = []
        head_sums = []
        up_sums = []
        next_bases = []
        next_ups = []
        down_job = (ups[0] + ups[1], [saved[layer][batch][7] for batch in everyone])
        if layer == 1:
            down_grad = weight_grad([down_job])
            down_sum = scatter_rows(down_grad)
        terms = []
        for batch in everyone:
            slope = saved[layer][batch][8]
            slope = after(slope, down_grad if layer == 1 else (first_sum, heads_grad))
            hidden_grad, hidden_sum, parts = feed_backward(ups[batch], up, down, slope, cols)
            hidden_grads.append(hidden_grad)
            up_sums.append(hidden_sum[0])
            terms.append(link.exchange(parts))
        if layer == 0:
            down_grad = weight_grad([(after(down_job[0], hidden_grads), down_job[1])])
            down_sum = scatter_rows(down_grad)
        middle_grads = []
        seconds = []
        for batch in everyone:
            middle = saved[layer][batch][5]
            middle_grad, half, second_sums = norm_backward(
                terms[batch], middle, bases[batch], gain_two, False,
                layer * 15000000000 + (1 - layer) * 15000000000,
            )
            middle_grads.append(middle_grad)
            seconds.append(second_sums)
            mids.append(link.spread(half))
            if batch == 0:
                up_job = (saved[layer][0][6] + saved[layer][1][6], after(hidden_grads, half))
                up_grad = weight_grad([up_job])
                up_sum = scatter_rows(up_grad)
        terms = []
        for batch in everyone:
            qkv, lse = saved[layer][batch][2], saved[layer][batch][4]
            lse = after(lse, up_grad, reduced[1][2] if layer == 0 else ())
            qkv_grad, head_sum, parts = heads_backward(
                mids[batch], first, second, qkv, lse, mask, heads, cols,
                (1 - layer) * 15000000000,
            )
            qkv_grads.append(qkv_grad)
            head_sums.append(head_sum.reshape(-1))
            terms.append(link.exchange(parts))
        if layer == 0:
            heads_grad = all_heads_grad(qkv_grads)
        for batch in everyone:
            stream = saved[layer][batch][0]
            if layer == 0:
                stream = after(stream, heads_grad)
            stream_grad, half, first_sums = norm_backward(
                terms[batch], stream, middle_grads[batch], gain_one, layer == 0, layer * 15000000000
            )
            second_sums = seconds[batch]
            next_bases.append(stream_grad)
            if layer == 1:
                next_ups.append(link.spread(half))
                if batch == 0:
                    heads_grad = all_heads_grad(after(qkv_grads, half))
            else:
                turned.append(half)
            sums.append((first_sums, second_sums))
        wide_sum = jnp.concatenate([down_sum, up_sum], axis=1)
        first_sum = (down_sum, up_sum) if layer == 1 else None
        if layer == 0:
            heads_grad = after(heads_grad, down_sum, up_sum, turned)
        reduced[layer] = (wide_sum, up_sum, scatter_rows(heads_grad))
        first_sums = sums[0][0] + sums[1][0]
        second_sums = sums[0][1] + sums[1][1]
        wide_sums[layer] = jnp.concatenate(
            [first_sums[:2], second_sums[2:3], second_sums[:2], base_sum], axis=0
        )
        base_sum = first_sums[2:3]
        narrow_sums[layer] = jnp.concatenate(
            [head_sums[0] + head_sums[1], up_sums[0] + up_sums[1]]
        )
        bases = next_bases
        ups = next_ups


    last_parts = feed_last(
        after([saved[1][batch][7] for batch in everyone], turned),
        [saved[1][batch][5] for batch in everyone],
        smalls[1][0][5],
        weights[1][3],
    )
    outputs = []
    last_terms = [link.exchange(last_parts[batch]) for batch in everyone]
    for terms in last_terms:
        outputs.append(sum([term.astype(F32) for term in terms[1:]], terms[0].astype(F32)))
    outputs = jnp.stack(outputs).astype(BF)

    wide_sums = after(wide_sums, last_terms[0])
    wide_both = jnp.stack(wide_sums).reshape(2, 6, cols, width)
    wide_here = lax.dynamic_index_in_dim(wide_both, col, 2, keepdims=False)
    for j in range(1, cols):
        wide_here = wide_here + xor_step(
            lax.dynamic_index_in_dim(wide_both, col ^ j, 2, keepdims=False), "col", j
        )
    small_sums = jnp.concatenate([wide_here.reshape(2, -1), jnp.stack(narrow_sums)], axis=1)
    small_own = lax.dynamic_index_in_dim(small_sums, section, 0, keepdims=False)
    small_own = small_own + swap_section(
        lax.dynamic_index_in_dim(small_sums, 1 - section, 0, keepdims=False)
    )
    step = 1
    while step < lax.axis_size("row"):
        small_own = small_own + xor_step(small_own, "row", step)
        step *= 2
    small_own = after(small_own, reduced[0][2])
    small_out = small_own[: 6 * width].reshape(6, width)
    head_out = small_own[6 * width : 6 * width + 2 * wide].reshape(2, wide)
    head_out = split_heads(
        head_out, previous_column(tail_columns(head_out, width, col)), width, col
    )
    up_bias_grad = small_own[6 * width + 2 * wide :]

    def settle(first_half, second_half):
        got = swap_section(jnp.where(is_first, second_half, first_half))
        keep = jnp.where(is_first, first_half, second_half)
        low = jnp.where(is_first, keep, got)
        high = jnp.where(is_first, got, keep)
        return jnp.concatenate([low, high], axis=0)

    wide_out = settle(reduced[0][0], reduced[1][0])
    down_out = wide_out[:, : wide_out.shape[1] // 2].astype(F32)
    up_out = wide_out[:, wide_out.shape[1] // 2 :].astype(F32)

    def by_matrix(flat):
        return jnp.stack([flat[:, i * wide : (i + 1) * wide] for i in range(4)])

    keep = by_matrix(jnp.where(is_first, reduced[0][2], reduced[1][2]))
    send = by_matrix(jnp.where(is_first, reduced[1][2], reduced[0][2]))
    got = swap_section(send)
    keep_before = previous_column(tail_columns(keep, width, col))
    got_before = previous_column_across(tail_columns(send, width, col))
    keep = split_heads(keep, keep_before, width, col)
    got = split_heads(got, got_before, width, col)
    heads_out = jnp.concatenate(
        [jnp.where(is_first, keep, got), jnp.where(is_first, got, keep)], axis=1
    ).astype(F32)

    grads = to_features(turned)
    outputs, grads = after((outputs, grads), reduced[0][2])
    got = swap_section(jnp.where(is_first, outputs, grads))
    keep = jnp.where(is_first, grads, outputs)
    boundary = jnp.concatenate(
        [jnp.where(is_first, keep, got), jnp.where(is_first, got, keep)], axis=0
    ).astype(F32)

    return (
        boundary[None],
        small_out[0][None],
        small_out[1][None],
        heads_out[0][None],
        heads_out[1][None],
        heads_out[2][None],
        head_out[0][None],
        head_out[1][None],
        heads_out[3].T[None],
        small_out[2][None],
        small_out[3][None],
        small_out[4][None],
        up_out[None],
        up_bias_grad[None],
        down_out[None],
        small_out[5][None],
    )


def solution(mesh):
    vector = P("section", "col")
    matrix = P("section", "row", "col")
    turned = P("section", "col", "row")
    plane = P(None, "col", "row")
    in_specs = (
        plane, plane, P(), vector, vector, matrix, matrix, matrix, vector, vector,
        turned, vector, vector, vector, matrix, vector, matrix, vector,
    )
    out_specs = (
        P("section", None, "col", "row"), vector, vector, matrix, matrix, matrix, vector, vector,
        turned, vector, vector, vector, matrix, vector, matrix, vector,
    )
    return jax.shard_map(
        on_device, mesh=mesh, in_specs=in_specs, out_specs=out_specs, check_vma=False
    )
```
